128 devices in a mesh: row: 32 (over z, x, core), col: 4 (over y).
Axes of the slice: x: 4, y: 4, z: 4, core: 2. Of those that a mesh axis runs over, the one named last changes fastest.
Arguments:
- grid_in: bfloat16 [16384, 227], P(('row', 'col')), may hold values from -6 to 6
- mesh_init: bfloat16 [40960, 512], P(('row', 'col')), may hold values from -6 to 6
- embed_first: bfloat16 [227, 512], replicated, may hold values from -0.375 to 0.375
- embed_second: bfloat16 [512, 512], replicated, may hold values from -0.25 to 0.25
- embed_gain: float32 [512], replicated, may hold values from 0.1 to 1.9
- edge_first: bfloat16 [4, 2, 512, 512], replicated, may hold values from -0.1875 to 0.1875
- edge_second: bfloat16 [4, 512, 512], replicated, may hold values from -0.25 to 0.25
- edge_gain: float32 [4, 512], replicated, may hold values from 0.1 to 1.9
- node_first: bfloat16 [4, 2, 512, 512], replicated, may hold values from -0.1875 to 0.1875
- node_second: bfloat16 [4, 512, 512], replicated, may hold values from -0.25 to 0.25
- node_gain: float32 [4, 512], replicated, may hold values from 0.1 to 1.9
- out_weight: bfloat16 [512, 227], replicated, may hold values from -0.25 to 0.25
- enc_send: int32 [128, 9, 128], P(('row', 'col')), may hold values from 0 to 127
- enc_slot: int32 [128, 768], P(('row', 'col')), may hold values from 0 to 1151, as said below
- enc_recv: int32 [128, 768], P(('row', 'col')), may hold values from 0 to 319, never falling along the last dimension, each value on 1 to 4 neighbouring positions
- proc_send: int32 [128, 9, 256], P(('row', 'col')), may hold values from 0 to 319
- proc_slot: int32 [128, 1600], P(('row', 'col')), may hold values from 0 to 4351, as said below
- proc_recv: int32 [128, 1600], P(('row', 'col')), may hold values from 0 to 319, never falling along the last dimension, each value on 1 to 10 neighbouring positions
- dec_send: int32 [128, 9, 64], P(('row', 'col')), may hold values from 0 to 319
- dec_slot: int32 [128, 384], P(('row', 'col')), may hold values from 0 to 575, as said below
- dec_recv: int32 [128, 384], P(('row', 'col')), may hold values from 0 to 127, never falling along the last dimension, each value on 1 to 6 neighbouring positions
Outputs:
- prediction: float32 [16384, 227], P(('row', 'col'))
The draws below stay inside these ranges and needn't reach their ends.
Inputs may be any that keep to these rules, and one draw needn't show every extreme that they name: `enc_slot`: no two edges of a device share a slot; no slot names a sender band outside 0 .. 31; in the first and the last band every other slot carries an edge. `proc_slot`: values under 9 * 256 are slots as for the other lists: distinct within a device, never naming a sender band outside 0 .. 31, all others used in the first and the last band; exactly 64 edges of each device have values from 2304 on. `dec_slot`: no two edges of a device share a slot; no slot names a sender band outside 0 .. 31; in the first and the last band every other slot carries an edge. `enc_recv`: Non-decreasing along each row; every local mesh node receives 1 to 4 edges. `proc_recv`: Non-decreasing along each row; every local mesh node receives 1 to 10 edges. `dec_recv`: Non-decreasing along each row; every local grid node receives 1 to 6 edges.
All inputs are finite; a program needn't handle non-finite values.
Results may differ from the reference program's by a relative error of at most 0.014.
Values may be sent and summed in bfloat16 or wider, within the bound.
A program may use at most 128 MiB of HBM per device.

```python
import math
from functools import partial
import jax
import jax.numpy as jnp
import numpy as np
from jax import lax

L = 512
CIN = 227
G_DEV = 128
MESH_DEV = 320
CAP_E = 128
CAP_M = 256
FAR_M = 64
COARSE_DEV = 16
SHARDS = 128
EG_DEV = 768
EM_DEV = 1600
CAP_D = 64
DE_DEV = 384
COARSE = 2048
GRID = 16384
MESH = 40960
N_ROW = 32
N_COL = 4


def pick_slots(key, capacity, count):
    owner = jnp.arange(SHARDS, dtype=jnp.int32)
    band = owner // N_COL
    slots = jnp.arange(9 * capacity, dtype=jnp.int32)
    lift = slots // capacity // 3 - 1
    source_band = band[:, None] - lift[None, :]
    beyond = ((source_band < 0) | (source_band > N_ROW - 1)).astype(jnp.int32)
    orders = jax.vmap(partial(jax.random.permutation, x=9 * capacity))(jax.random.split(key, SHARDS))
    scores = orders.astype(jnp.int32) + beyond * (9 * capacity)
    ranked = jnp.argsort(scores, axis=1, stable=True)
    return ranked[:, :count].astype(jnp.int32)


def draw_enc_slot(key, part):
    key = jax.random.fold_in(key, 11)
    return pick_slots(key, CAP_E, EG_DEV)


def draw_dec_slot(key, part):
    key = jax.random.fold_in(key, 13)
    return pick_slots(key, CAP_D, DE_DEV)


def draw_proc_slot(key, part):
    key = jax.random.fold_in(key, 17)
    near_key, far_key, mix_key = jax.random.split(key, 3)
    nearby = pick_slots(near_key, CAP_M, 6 * CAP_M)
    distant = jax.random.randint(far_key, (SHARDS, FAR_M), 0, COARSE, dtype=jnp.int32) + 9 * CAP_M
    distant = distant.at[0, 0].set(9 * CAP_M + COARSE - 1)
    joined = jnp.concatenate([nearby, distant], axis=1)
    orders = jax.vmap(partial(jax.random.permutation, x=EM_DEV))(jax.random.split(mix_key, SHARDS))
    return jnp.take_along_axis(joined, orders.astype(jnp.int32), axis=1).astype(jnp.int32)


def set_ends(values, own_key, least, top_value):
    shape = values.shape
    index_at = [jax.random.randint(jax.random.fold_in(own_key, axis), (), 0, shape[axis]) for axis in range(len(shape))]
    values = values.at[tuple(index_at)].set(least)
    longest = shape.index(max(shape))
    index_at[longest] = (index_at[longest] + 1) % shape[longest]
    return values.at[tuple(index_at)].set(top_value)


def shard_levels(stream_key, extent, cuts, low, largest):
    def one(axis_at, blocks):
        heights = jax.random.uniform(jax.random.fold_in(jax.random.fold_in(stream_key, 6), axis_at), (blocks,), jnp.float32, low / len(cuts), largest / len(cuts))
        return jnp.repeat(jnp.exp(heights), extent[axis_at] // blocks).reshape((-1,) + (1,) * (len(extent) - axis_at - 1))

    level = one(*cuts[0])
    for cut in cuts[1:]:
        level = level * one(*cut)
    return level


def profile(amount, total, limit, lean):
    portions = [(1 << 20) // math.isqrt(standing ** lean) + 1 for standing in range(2, amount + 1)]
    spare, counts = total - limit - (amount - 1), [1] * (amount - 1)
    while spare > 0:
        candidates = [i for i in range(amount - 1) if counts[i] < limit]
        pool, remaining = sum([portions[i] for i in candidates]), spare
        for i in candidates:
            extra = min(limit - counts[i], max(1, remaining * portions[i] // pool), spare)
            counts[i] = counts[i] + extra
            spare = spare - extra
    return np.array([limit] + counts)


def ragged_sizes(rng, amount, total, most, lean):
    if amount == 2:
        one = jax.random.randint(rng, (), max(1, total - most), min(most, total - 1) + 1)
        return jnp.stack([one, total - one])
    sizes = jnp.asarray(profile(amount, total, most, lean), jnp.int32)
    pairs = (amount - 1) // 2
    donor, receiver = sizes[1:1 + 2 * pairs:2], sizes[2:2 + 2 * pairs:2]
    room = jnp.minimum(donor - 1, most - receiver)
    moved = jax.random.randint(jax.random.fold_in(rng, 1), (pairs,), 0, 1 << 20) % (room + 1)
    sizes = sizes.at[1:1 + 2 * pairs:2].set(donor - moved).at[2:2 + 2 * pairs:2].set(receiver + moved)
    return sizes[jax.random.permutation(jax.random.fold_in(rng, 2), amount)]


def gaussian(stream_key, extent, scale, limit, shards=(), kind=jnp.bfloat16):
    loudness = shard_levels(stream_key, extent, shards, -0.22, 0.18) if shards else 1.0
    result = jax.random.normal(stream_key, extent, jnp.float32) * scale * loudness
    return jnp.minimum(jnp.maximum(result, -limit), limit).astype(kind)


def setup_inputs(seed: int = 0) -> dict:
    key_list = jax.random.split(jax.random.key(seed), 22)
    return {
        "grid_in": gaussian(key_list[0], (GRID, CIN), 1.0, 6.0, ((0, 128),)),
        "mesh_init": gaussian(key_list[1], (MESH, L), 1.0, 6.0, ((0, 128),)),
        "embed_first": gaussian(key_list[2], (CIN, L), CIN ** -0.5, 0.375),
        "embed_second": gaussian(key_list[3], (L, L), L ** -0.5, 0.25),
        "embed_gain": jnp.clip(1.0 + 0.18 * jax.random.normal(key_list[4], (L,), jnp.float32), 0.1, 1.9),
        "edge_first": gaussian(key_list[5], (4, 2, L, L), (2 * L) ** -0.5, 0.1875),
        "edge_second": gaussian(key_list[6], (4, L, L), L ** -0.5, 0.25),
        "edge_gain": jnp.clip(1.0 + 0.18 * jax.random.normal(key_list[7], (4, L), jnp.float32), 0.1, 1.9),
        "node_first": gaussian(key_list[8], (4, 2, L, L), (2 * L) ** -0.5, 0.1875),
        "node_second": gaussian(key_list[9], (4, L, L), L ** -0.5, 0.25),
        "node_gain": jnp.clip(1.0 + 0.18 * jax.random.normal(key_list[10], (4, L), jnp.float32), 0.1, 1.9),
        "out_weight": gaussian(key_list[11], (L, CIN), L ** -0.5, 0.25),
        "enc_send": set_ends(jax.random.randint(key_list[12], (SHARDS, 9, CAP_E), 0, G_DEV), jax.random.fold_in(key_list[12], 1), 0, G_DEV - 1).astype(jnp.int32),
        "enc_slot": draw_enc_slot(jax.random.fold_in(key_list[21], 71), 0),
        "enc_recv": jax.vmap(lambda own: jnp.searchsorted(jnp.cumsum(ragged_sizes(own, MESH_DEV, EG_DEV, 2 * EG_DEV // MESH_DEV, 2)), jnp.arange(EG_DEV), side="right"))(jax.random.split(key_list[14], SHARDS)).reshape((SHARDS, EG_DEV)).astype(jnp.int32),
        "proc_send": set_ends(jax.random.randint(key_list[15], (SHARDS, 9, CAP_M), 0, MESH_DEV), jax.random.fold_in(key_list[15], 1), 0, MESH_DEV - 1).astype(jnp.int32),
        "proc_slot": draw_proc_slot(jax.random.fold_in(key_list[21], 71), 0),
        "proc_recv": jax.vmap(lambda own: jnp.searchsorted(jnp.cumsum(ragged_sizes(own, MESH_DEV, EM_DEV, 2 * EM_DEV // MESH_DEV, 2)), jnp.arange(EM_DEV), side="right"))(jax.random.split(key_list[17], SHARDS)).reshape((SHARDS, EM_DEV)).astype(jnp.int32),
        "dec_send": set_ends(jax.random.randint(key_list[18], (SHARDS, 9, CAP_D), 0, MESH_DEV), jax.random.fold_in(key_list[18], 1), 0, MESH_DEV - 1).astype(jnp.int32),
        "dec_slot": draw_dec_slot(jax.random.fold_in(key_list[21], 71), 0),
        "dec_recv": jax.vmap(lambda own: jnp.searchsorted(jnp.cumsum(ragged_sizes(own, G_DEV, DE_DEV, 6, 2)), jnp.arange(DE_DEV), side="right"))(jax.random.split(key_list[20], SHARDS)).reshape((SHARDS, DE_DEV)).astype(jnp.int32),
    }


EPSILON = 1e-05

def layer_norm(values, gain):
    average = lax.optimization_barrier(jnp.mean(values, axis=-1, keepdims=True))
    centered = values - average
    spread_sq = lax.optimization_barrier(jnp.mean(centered * centered, axis=-1, keepdims=True))
    return centered * lax.rsqrt(spread_sq + EPSILON) * gain.astype(jnp.float32)

def perceptron(inputs, firsts, second, gain):
    summed = jnp.dot(inputs[0], firsts[0], preferred_element_type=jnp.float32)
    for part_in, weight in zip(inputs[1:], firsts[1:]):
        summed = summed + jnp.dot(part_in, weight, preferred_element_type=jnp.float32)
    hidden = jax.nn.silu(summed).astype(jnp.bfloat16)
    return layer_norm(jnp.dot(hidden, second, preferred_element_type=jnp.float32), gain)

def sender_rows(send, slot, capacity, row_count):
    owner = jnp.arange(SHARDS, dtype=jnp.int32)[:, None] * jnp.ones_like(slot)
    band = owner // N_COL
    sector = owner % N_COL
    nearby = jnp.minimum(slot, 9 * capacity - 1)
    block = nearby // capacity
    position = nearby % capacity
    source_band = jnp.clip(band - (block // 3 - 1), 0, N_ROW - 1)
    source_sector = (sector - (block % 3 - 1)) % N_COL
    source = (source_band * N_COL + source_sector).astype(jnp.int32)
    near_row = source * row_count + send[source, block, position]
    coarse_id = jnp.maximum(slot - 9 * capacity, 0)
    far_row = coarse_id // COARSE_DEV * MESH_DEV + coarse_id % COARSE_DEV
    return jnp.where(slot >= 9 * capacity, far_row, near_row).astype(jnp.int32)

def interact(section_id, senders, receivers, sender_index, recv, recv_rows, edge_first, edge_second, edge_gain, node_first, node_second, node_gain):

    def per_device(items):
        device, picked, local = items
        block = lax.dynamic_slice_in_dim(receivers, device * recv_rows, recv_rows, 0)
        sent = jnp.take(senders, picked, axis=0)
        there = jnp.take(block, local, axis=0)
        message = perceptron([sent, there], [edge_first[section_id, 0], edge_first[section_id, 1]], edge_second[section_id], edge_gain[section_id]).astype(jnp.bfloat16)
        onehot = (local[None, :] == jnp.arange(recv_rows, dtype=jnp.int32)[:, None]).astype(jnp.bfloat16)
        summed = jnp.dot(onehot, message, preferred_element_type=jnp.float32).astype(jnp.bfloat16)
        update = perceptron([block, summed], [node_first[section_id, 0], node_first[section_id, 1]], node_second[section_id], node_gain[section_id])
        return (block.astype(jnp.float32) + update).astype(jnp.bfloat16)
    blocks = lax.map(per_device, (jnp.arange(SHARDS, dtype=jnp.int32), sender_index, recv))
    return blocks.reshape(SHARDS * recv_rows, receivers.shape[1])

def reference(grid_in, mesh_init, embed_first, embed_second, embed_gain, edge_first, edge_second, edge_gain, node_first, node_second, node_gain, out_weight, enc_send, enc_slot, enc_recv, proc_send, proc_slot, proc_recv, dec_send, dec_slot, dec_recv):
    weights = (edge_first, edge_second, edge_gain, node_first, node_second, node_gain)
    grid_latent = perceptron([grid_in], [embed_first], embed_second, embed_gain).astype(jnp.bfloat16)
    enc_index = sender_rows(enc_send, enc_slot, CAP_E, G_DEV)
    proc_index = sender_rows(proc_send, proc_slot, CAP_M, MESH_DEV)
    dec_index = sender_rows(dec_send, dec_slot, CAP_D, MESH_DEV)
    mesh_latent = interact(0, grid_latent, mesh_init, enc_index, enc_recv, MESH_DEV, *weights)
    mesh_latent = interact(1, mesh_latent, mesh_latent, proc_index, proc_recv, MESH_DEV, *weights)
    mesh_latent = interact(2, mesh_latent, mesh_latent, proc_index, proc_recv, MESH_DEV, *weights)
    grid_final = interact(3, mesh_latent, grid_latent, dec_index, dec_recv, G_DEV, *weights)
    return grid_in.astype(jnp.float32) + jnp.dot(grid_final, out_weight, preferred_element_type=jnp.float32)
```

```python
import functools

import jax
import jax.numpy as jnp
from jax import lax
from jax.experimental import pallas as pl
from jax.experimental.pallas import tpu as pltpu
from jax.sharding import PartitionSpec as P

BF = jnp.bfloat16
F32 = jnp.float32
I32 = jnp.int32
MESH = pl.DeviceIdType.MESH

L = 512
CIN = 227
G = 128
N = 320
CO = 16
FAR = 64
CE, CM, CD = 128, 256, 64
EE, EM, ED = 768, 1600, 384
EMP = 1664
FIRST_FAR = 9 * CM
EPSILON = 1e-05

ORDER = (4, 1, 7, 3, 5, 0, 2, 6, 8)
PLACE = {b: k for k, b in enumerate(ORDER)}


def dot(a, b):
    return jnp.dot(a, b, preferred_element_type=F32)


def dot_nt(a, b):
    return lax.dot_general(a, b, (((1,), (1,)), ((), ())), preferred_element_type=F32)


def iota(shape, dim):
    return lax.broadcasted_iota(I32, shape, dim)


def ones_where(cond):
    return jnp.where(cond, 1.0, 0.0).astype(BF)


def silu(v):
    u = 0.5 * v
    return (u + u * jnp.tanh(u)).astype(BF)


def layer_norm(y, gain):
    average = jnp.mean(y, axis=-1, keepdims=True)
    centered = y - average
    spread = jnp.mean(centered * centered, axis=-1, keepdims=True)
    return centered * lax.rsqrt(spread + EPSILON) * gain


def slot_receivers(slot, recv, high):
    edges = slot.shape[1]
    at_high = (slot >> 7) == iota((high, edges), 0)
    code = recv + 1
    first = jnp.where(at_high, (code >> 6).astype(F32), 0.0).astype(BF)
    second = jnp.where(at_high, (code & 63).astype(F32), 0.0).astype(BF)
    at_low = ones_where((slot & 127) == iota((128, edges), 0))
    rows = dot_nt(first, at_low) * 64.0 + dot_nt(second, at_low) - 1.0
    cols = dot_nt(at_low, first) * 64.0 + dot_nt(at_low, second) - 1.0
    return rows.astype(I32), cols.astype(I32)


def body(
    nr,
    nc,
    grid_in,
    mesh_init,
    embed_first,
    embed_second,
    embed_gain,
    edge_first_any,
    edge_second_any,
    edge_gain,
    node_first_any,
    node_second_any,
    node_gain,
    out_weight,
    enc_send,
    enc_slot,
    enc_recv,
    proc_send,
    proc_slot,
    proc_recv,
    dec_send,
    dec_slot,
    dec_recv,
    out,
    ef,
    es,
    nf,
    ns,
    tab_out,
    tab_in,
    tab_t,
    far_out,
    far_in,
    slot_pad,
    recv_pad,
    slot_2d,
    enc_halo,
    enc_w,
    enc_m,
    proc_halo,
    proc_w,
    proc_m,
    far_e,
    far_m,
    gath,
    c_out,
    c_in,
    dec_out,
    dec_in,
    dec_g,
    dec_e,
    dec_m,
    grid_lat,
    lat,
    base,
    agg,
    w_sem,
    tab_ss,
    tab_rs,
    far_ss,
    far_rs,
    halo_ss,
    halo_rs,
    g_ss,
    g_rs,
    p_ss,
    p_rs,
    y_ss,
    y_rs,
    d_ss,
    d_rs,
):
    nzx = nr // 2
    r = lax.axis_index("row")
    c = lax.axis_index("col")
    core = lax.rem(r, 2)
    zx = r // 2
    up, down = lax.rem(r + 1, nr), lax.rem(r + nr - 1, nr)
    right, left = lax.rem(c + 1, nc), lax.rem(c + nc - 1, nc)
    rows_of = {-1: down, 0: r, 1: up}
    cols_of = {-1: left, 0: c, 1: right}
    partner = r + 1 - 2 * core

    def target(b):
        return (rows_of[b // 3 - 1], cols_of[b % 3 - 1])

    def peer(d):
        return (lax.rem(zx + d, nzx) * 2 + core, c)

    def mate(i):
        return (r, lax.rem(c + nc - i, nc))

    others = [b for b in range(9) if b != 4]

    barrier = pltpu.get_barrier_semaphore()
    greeted = [target(b) for b in others] + [peer(d) for d in range(1, nzx)] + [mate(2)]
    for device in greeted:
        pl.semaphore_signal(barrier, inc=1, device_id=device, device_id_type=MESH)

    weight_copies = []
    for i in range(4):
        group = []
        for j, (source, place) in enumerate(
            (
                (edge_first_any, ef),
                (edge_second_any, es),
                (node_first_any, nf),
                (node_second_any, ns),
            )
        ):
            copy = pltpu.make_async_copy(source.at[i], place.at[i], w_sem.at[i, j])
            copy.start()
            group.append(copy)
        weight_copies.append(group)

    for b in range(9):
        tab_out[b, 0:1, :] = enc_send[0, b : b + 1, :]
        tab_out[b, 1:2, :] = proc_send[0, b : b + 1, 0:128]
        tab_out[b, 2:3, :] = proc_send[0, b : b + 1, 128:256]
        tab_out[b, 3:8, :] = jnp.zeros((5, 128), I32)
    tab_in[0] = tab_out[4]

    hidden = silu(dot(grid_in[...], embed_first[...]))
    latent = layer_norm(dot(hidden, embed_second[...]), embed_gain[...]).astype(BF)
    grid_lat[...] = latent
    weight_copies[0][0].wait()
    enc_halo[0, 0:G, :] = dot(latent, ef[0, 0]).astype(BF)

    pl.semaphore_wait(barrier, len(greeted))

    tab_copies = []
    for b in others:
        k = PLACE[b]
        copy = pltpu.make_async_remote_copy(
            tab_out.at[b], tab_in.at[k], tab_ss.at[k], tab_rs.at[k],
            device_id=target(b), device_id_type=MESH,
        )
        copy.start()
        tab_copies.append(copy)

    def halo_copy(step, halo, size, src, dst):
        b = ORDER[dst]
        dr, dc = b // 3 - 1, b % 3 - 1
        if src != 0:
            dc = 0
        return pltpu.make_async_remote_copy(
            halo.at[src, pl.ds(0, size)],
            halo.at[dst, pl.ds(0, size)],
            halo_ss.at[step, dst],
            halo_rs.at[step, dst],
            device_id=(rows_of[dr], cols_of[dc]),
            device_id_type=MESH,
        )

    def halo_direct(step, halo, size):
        copies = {}
        for b in (3, 5, 1, 7):
            k = PLACE[b]
            copies[k] = halo_copy(step, halo, size, 0, k)
            copies[k].start()
        return copies

    def halo_forward(step, halo, size, copies):
        for here, onward in ((3, (0, 6)), (5, (2, 8))):
            copies[PLACE[here]].wait_recv()
            for b in onward:
                k = PLACE[b]
                copies[k] = halo_copy(step, halo, size, PLACE[here], k)
                copies[k].start()

    def slot_messages(step, halo, w, m, i, k):
        pre = dot(w[k], halo[k])
        y = dot(silu(pre), es[i])
        message = layer_norm(y, edge_gain[i : i + 1, :]).astype(BF)
        agg[...] += dot(m[k], message)

    def node_update(i, own, summed, start):
        node = start + dot(summed.astype(BF), nf[i, 1])
        update = layer_norm(dot(silu(node), ns[i]), node_gain[i : i + 1, :])
        return (own.astype(F32) + update).astype(BF)

    copies = halo_direct(0, enc_halo, G)

    receiver_part = dot(mesh_init[...], ef[0, 1]).astype(BF)
    for k in range(9):
        enc_halo[k, G : G + N, :] = receiver_part

    slot_pad[...] = jnp.full((1, EMP), -1, I32)
    recv_pad[...] = jnp.zeros((1, EMP), I32)
    slot_pad[0:1, 0:EM] = proc_slot[...]
    recv_pad[0:1, 0:EM] = proc_recv[...]
    slot_2d[...] = jnp.full((16, 128), -1, I32)
    chunks = EMP // 128
    for i in range(chunks):
        slot_2d[i : i + 1, :] = slot_pad[0:1, i * 128 : (i + 1) * 128]
    is_far = slot_2d[...] >= FIRST_FAR
    far_ones = ones_where(is_far)
    within = dot(far_ones, ones_where(iota((128, 128), 0) <= iota((128, 128), 1)))
    above = dot(ones_where(iota((16, 16), 1) < iota((16, 16), 0)), far_ones)
    rank = within + jnp.sum(above, axis=1, keepdims=True) - 1.0
    rank = jnp.where(is_far, rank.astype(I32), -1)
    picks = jnp.concatenate(
        [ones_where(rank[i : i + 1, :] == iota((FAR, 128), 0)) for i in range(chunks)], axis=1
    )
    node = jnp.maximum(slot_pad[...] - FIRST_FAR, 0)
    row_id = iota((8, EMP), 0)
    values = jnp.where(
        row_id == 0,
        node >> 6,
        jnp.where(
            row_id == 1,
            node & 63,
            jnp.where(row_id == 2, recv_pad[...] >> 6, jnp.where(row_id == 3, recv_pad[...] & 63, 0)),
        ),
    )
    values = values.astype(F32).astype(BF)
    far_cols = dot_nt(picks, values)
    far_rows = dot_nt(values, picks)
    far_node = (far_cols[:, 0:1] * 64.0 + far_cols[:, 1:2]).astype(I32)
    far_out[...] = jnp.broadcast_to(far_node, (FAR, 128))
    far_in[0] = jnp.broadcast_to(far_node, (FAR, 128))
    far_copies = []
    for i in range(1, nc):
        copy = pltpu.make_async_remote_copy(
            far_out, far_in.at[nc - i], far_ss.at[nc - i], far_rs.at[nc - i],
            device_id=mate(i), device_id_type=MESH,
        )
        copy.start()
        far_copies.append(copy)
    far_recv_col = (far_cols[:, 2:3] * 64.0 + far_cols[:, 3:4]).astype(I32)
    far_recv_row = (far_rows[2:3, :] * 64.0 + far_rows[3:4, :]).astype(I32)
    far_e[...] = ones_where(far_recv_col == iota((FAR, N), 1))
    far_m[...] = ones_where(far_recv_row == iota((N, FAR), 0))

    enc_rows, enc_cols = slot_receivers(enc_slot[...], enc_recv[...], 16)
    for copy in tab_copies:
        copy.wait_recv()
    tab_t[0:72, :] = tab_in[...].reshape(72, 128).astype(F32)
    tab_t[72:128, :] = jnp.zeros((56, 128), F32)
    tabs = jnp.transpose(tab_t[...]).astype(I32)
    for k in range(9):
        b = ORDER[k]
        at = iota((CE, G + N), 1)
        receiver = enc_cols[:, b : b + 1]
        receiver = jnp.where(receiver < 0, -1, receiver + G)
        enc_w[k] = ones_where((at == tabs[:, 8 * k : 8 * k + 1]) | (at == receiver))
        enc_m[k] = ones_where(enc_rows[b : b + 1, :] == iota((N, CE), 0))

    weight_copies[0][1].wait()
    agg[...] = jnp.zeros((N, L), F32)
    slot_messages(0, enc_halo.at[:], enc_w, enc_m, 0, 0)
    halo_forward(0, enc_halo, G, copies)
    weight_copies[0][2].wait()
    weight_copies[0][3].wait()
    base[...] = dot(mesh_init[...], nf[0, 0])

    proc_rows, proc_cols = slot_receivers(slot_pad[...], recv_pad[...], 24)
    for k in range(9):
        b = ORDER[k]
        at = iota((128, 2 * N), 1)
        for half in range(2):
            h = 2 * b + half
            receiver = proc_cols[:, h : h + 1]
            receiver = jnp.where(receiver < 0, -1, receiver + N)
            sender = tabs[:, 8 * k + 1 + half : 8 * k + 2 + half]
            span = slice(half * 128, (half + 1) * 128)
            proc_w[k, span, :] = ones_where((at == sender) | (at == receiver))
            proc_m[k, :, span] = ones_where(proc_rows[h : h + 1, :] == iota((N, 128), 0))

    dec_rows, dec_cols = slot_receivers(dec_slot[...], dec_recv[...], 16)
    for h in range(5):
        span = slice(h * 128, (h + 1) * 128)
        dec_e[span, :] = ones_where(dec_cols[:, h : h + 1] == iota((128, G), 1))
        dec_m[:, span] = ones_where(dec_rows[h : h + 1, :] == iota((G, 128), 0))
    tab_t[...] = jnp.zeros((128, 128), F32)
    tab_t[0:9, 0:CD] = dec_send[0].astype(F32)
    dec_tabs = jnp.transpose(tab_t[...]).astype(I32)
    for b in range(9):
        dec_g[b * CD : (b + 1) * CD, :] = ones_where(dec_tabs[0:CD, b : b + 1] == iota((CD, N), 1))
    dec_in[9 * CD : 640, :] = jnp.zeros((64, L), BF)

    @pl.loop(1, 3)
    def _(k):
        halo_wait(0, enc_halo, G, halo_rs, k)
        slot_messages(0, enc_halo, enc_w, enc_m, 0, k)

    @pl.loop(3, 5)
    def _(k):
        slot_messages(0, enc_halo, enc_w, enc_m, 0, k)

    @pl.loop(5, 9)
    def _(k):
        halo_wait(0, enc_halo, G, halo_rs, k)
        slot_messages(0, enc_halo, enc_w, enc_m, 0, k)

    lat[...] = node_update(0, mesh_init[...], agg[...], base[...])
    for copy in copies.values():
        copy.wait_send()
    for copy in tab_copies + far_copies:
        copy.wait_send()

    for s in range(2):
        i = s + 1
        halo = proc_halo.at[s]
        for copy in weight_copies[i]:
            copy.wait()
        own = lat[...]
        sent = dot(own, ef[i, 0]).astype(BF)
        halo[0, 0:N, :] = sent
        copies = halo_direct(i, halo, N)
        place = pl.multiple_of((core * nzx + zx) * CO, CO)
        gath[s, pl.ds(place, CO), :] = sent[0:CO, :]
        peer_copies = []
        for d in range(1, nzx):
            copy = pltpu.make_async_remote_copy(
                gath.at[s, pl.ds(place, CO)], gath.at[s, pl.ds(place, CO)],
                g_ss.at[s, d], g_rs.at[s, d], device_id=peer(d), device_id_type=MESH,
            )
            copy.start()
            peer_copies.append(copy)
        receiver_part = dot(own, ef[i, 1]).astype(BF)
        for k in range(9):
            halo[k, N : 2 * N, :] = receiver_part
        agg[...] = jnp.zeros((N, L), F32)
        slot_messages(i, halo, proc_w, proc_m, i, 0)
        halo_forward(i, halo, N, copies)

        for copy in peer_copies:
            copy.wait_recv()
        mine = pl.ds(pl.multiple_of(core * (nzx * CO), CO), nzx * CO)
        to_partner = pltpu.make_async_remote_copy(
            gath.at[s, mine], gath.at[s, mine], p_ss.at[s], p_rs.at[s],
            device_id=(partner, c), device_id_type=MESH,
        )
        to_partner.start()
        base[...] = dot(own, nf[i, 0])

        @pl.loop(1, 3)
        def _(k):
            halo_wait(i, halo, N, halo_rs, k)
            slot_messages(i, halo, proc_w, proc_m, i, k)

        to_partner.wait_recv()
        if s == 0:
            for copy in far_copies:
                copy.wait_recv()
        found = []
        for q in range(nc):
            number = far_in[q]
            device = number // CO
            band = device // nc
            index = (band % 2) * (nzx * CO) + (band // 2) * CO + number % CO
            index = jnp.where(device % nc == c, index, -1)
            found.append(
                jnp.concatenate(
                    [ones_where(index == iota((FAR, 128), 1) + 128 * t) for t in range(nr * CO // 128)],
                    axis=1,
                )
            )
        chosen = dot(jnp.concatenate(found, axis=0), gath[s]).astype(BF)
        c_out[s] = chosen
        mate_copies = []
        for q in range(1, nc):
            copy = pltpu.make_async_remote_copy(
                c_out.at[s, pl.ds(q * FAR, FAR)], c_in.at[s, q], y_ss.at[s, q], y_rs.at[s, q],
                device_id=mate(q), device_id_type=MESH,
            )
            copy.start()
            mate_copies.append(copy)

        @pl.loop(3, 5)
        def _(k):
            slot_messages(i, halo, proc_w, proc_m, i, k)

        @pl.loop(5, 9)
        def _(k):
            halo_wait(i, halo, N, halo_rs, k)
            slot_messages(i, halo, proc_w, proc_m, i, k)

        pre = c_out[s, 0:FAR, :].astype(F32) + dot(far_e[...], halo[0, N : 2 * N, :])
        for copy in mate_copies:
            copy.wait_recv()
        for q in range(1, nc):
            pre = pre + c_in[s, q].astype(F32)
        y = dot(silu(pre), es[i])
        message = layer_norm(y, edge_gain[i : i + 1, :]).astype(BF)
        summed = agg[...] + dot(far_m[...], message)
        lat[...] = node_update(i, own, summed, base[...])
        for copy in list(copies.values()) + peer_copies + mate_copies + [to_partner]:
            copy.wait_send()

    for copy in weight_copies[3]:
        copy.wait()
    sent = dot(lat[...], ef[3, 0]).astype(BF)
    dec_out[...] = dot(dec_g[...], sent).astype(BF)
    dec_copies = []
    for b in others:
        span = pl.ds(b * CD, CD)
        copy = pltpu.make_async_remote_copy(
            dec_out.at[span], dec_in.at[span], d_ss.at[b], d_rs.at[b],
            device_id=target(b), device_id_type=MESH,
        )
        copy.start()
        dec_copies.append(copy)
    dec_in[4 * CD : 5 * CD, :] = dec_out[4 * CD : 5 * CD, :]
    own = grid_lat[...]
    receiver_part = dot(own, ef[3, 1]).astype(BF)
    near = dot(dec_e[...], receiver_part)
    start = dot(own, nf[3, 0])
    for copy in dec_copies:
        copy.wait_recv()
    pre = dec_in[...].astype(F32) + near
    y = dot(silu(pre), es[3])
    message = layer_norm(y, edge_gain[3:4, :]).astype(BF)
    final = node_update(3, own, dot(dec_m[...], message), start)
    out[...] = grid_in[...].astype(F32) + dot(final, out_weight[...])
    for copy in dec_copies:
        copy.wait_send()


def halo_wait(step, halo, size, sems, k):
    pltpu.make_async_copy(halo.at[k, pl.ds(0, size)], halo.at[k, pl.ds(0, size)], sems.at[step, k]).wait()


def on_device(nr, nc, *args):
    vmem = pl.BlockSpec(memory_space=pltpu.VMEM)
    hbm = pl.BlockSpec(memory_space=pl.ANY)
    in_specs = [vmem] * 21
    for at in (5, 6, 8, 9):
        in_specs[at] = hbm
    args = list(args)
    args[4] = args[4].reshape(1, L)
    dma = pltpu.SemaphoreType.DMA
    nzx = nr // 2
    return pl.pallas_call(
        functools.partial(body, nr, nc),
        out_shape=jax.ShapeDtypeStruct((G, CIN), F32),
        in_specs=in_specs,
        out_specs=vmem,
        scratch_shapes=[
            pltpu.VMEM((4, 2, L, L), BF),
            pltpu.VMEM((4, L, L), BF),
            pltpu.VMEM((4, 2, L, L), BF),
            pltpu.VMEM((4, L, L), BF),
            pltpu.VMEM((9, 8, 128), I32),
            pltpu.VMEM((9, 8, 128), I32),
            pltpu.VMEM((128, 128), F32),
            pltpu.VMEM((FAR, 128), I32),
            pltpu.VMEM((nc, FAR, 128), I32),
            pltpu.VMEM((1, EMP), I32),
            pltpu.VMEM((1, EMP), I32),
            pltpu.VMEM((16, 128), I32),
            pltpu.VMEM((9, G + N, L), BF),
            pltpu.VMEM((9, CE, G + N), BF),
            pltpu.VMEM((9, N, CE), BF),
            pltpu.VMEM((2, 9, 2 * N, L), BF),
            pltpu.VMEM((9, CM, 2 * N), BF),
            pltpu.VMEM((9, N, CM), BF),
            pltpu.VMEM((FAR, N), BF),
            pltpu.VMEM((N, FAR), BF),
            pltpu.VMEM((2, nr * CO, L), BF),
            pltpu.VMEM((2, nc * FAR, L), BF),
            pltpu.VMEM((2, nc, FAR, L), BF),
            pltpu.VMEM((9 * CD, L), BF),
            pltpu.VMEM((640, L), BF),
            pltpu.VMEM((9 * CD, N), BF),
            pltpu.VMEM((640, G), BF),
            pltpu.VMEM((G, 640), BF),
            pltpu.VMEM((G, L), BF),
            pltpu.VMEM((N, L), BF),
            pltpu.VMEM((N, L), F32),
            pltpu.VMEM((N, L), F32),
            dma((4, 4)),
            dma((9,)),
            dma((9,)),
            dma((nc,)),
            dma((nc,)),
            dma((3, 9)),
            dma((3, 9)),
            dma((2, nzx)),
            dma((2, nzx)),
            dma((2,)),
            dma((2,)),
            dma((2, nc)),
            dma((2, nc)),
            dma((9,)),
            dma((9,)),
        ],
        compiler_params=pltpu.CompilerParams(
            collective_id=0, has_side_effects=True, vmem_limit_bytes=60 * 1024 * 1024
        ),
    )(*args)


def solution(mesh):
    both = ("row", "col")
    placed = (
        (P(both, None),) * 2
        + (P(),) * 10
        + (P(both, None, None), P(both, None), P(both, None)) * 3
    )
    return jax.shard_map(
        functools.partial(on_device, mesh.shape["row"], mesh.shape["col"]),
        mesh=mesh,
        in_specs=placed,
        out_specs=P(both, None),
        check_vma=False,
    )
```

```python
import functools

import jax
import jax.numpy as jnp
from jax import lax
from jax.experimental import pallas as pl
from jax.experimental.pallas import tpu as pltpu
from jax.sharding import PartitionSpec as P

BF = jnp.bfloat16
F32 = jnp.float32
I32 = jnp.int32
MESH = pl.DeviceIdType.MESH

L = 512
CIN = 227
G = 128
N = 320
CO = 16
FAR = 64
CE, CM, CD = 128, 256, 64
EE, EM, ED = 768, 1600, 384
EMP = 1664
FIRST_FAR = 9 * CM
EPSILON = 1e-05

CH = 80


def dot(a, b):
    return jnp.dot(a, b, preferred_element_type=F32)


def dot_nt(a, b):
    return lax.dot_general(a, b, (((1,), (1,)), ((), ())), preferred_element_type=F32)


def iota(shape, dim):
    return lax.broadcasted_iota(I32, shape, dim)


def ones_where(cond):
    return jnp.where(cond, 1.0, 0.0).astype(BF)


def silu(v):
    u = 0.5 * v
    return (u + u * jnp.tanh(u)).astype(BF)


def layer_norm(y, gain):
    average = jnp.mean(y, axis=-1, keepdims=True)
    centered = y - average
    spread = jnp.mean(centered * centered, axis=-1, keepdims=True)
    return centered * lax.rsqrt(spread + EPSILON) * gain


def slot_receivers(slot, recv, high):
    edges = slot.shape[1]
    at_high = (slot >> 7) == iota((high, edges), 0)
    code = recv + 1
    first = jnp.where(at_high, (code >> 6).astype(F32), 0.0).astype(BF)
    second = jnp.where(at_high, (code & 63).astype(F32), 0.0).astype(BF)
    at_low = ones_where((slot & 127) == iota((128, edges), 0))
    rows = dot_nt(first, at_low) * 64.0 + dot_nt(second, at_low) - 1.0
    cols = dot_nt(at_low, first) * 64.0 + dot_nt(at_low, second) - 1.0
    return rows.astype(I32), cols.astype(I32)


def body(
    nr,
    nc,
    grid_in,
    mesh_init,
    embed_first,
    embed_second,
    embed_gain,
    edge_first_any,
    edge_second_any,
    edge_gain,
    node_first_any,
    node_second_any,
    node_gain,
    out_weight,
    enc_send,
    enc_slot,
    enc_recv,
    proc_send,
    proc_slot,
    proc_recv,
    dec_send,
    dec_slot,
    dec_recv,
    out,
    ef,
    es,
    nf,
    ns,
    mesh_own,
    out_own,
    tab_out,
    tab_in,
    tab_t,
    far_out,
    far_in,
    slot_pad,
    recv_pad,
    slot_2d,
    enc_halo,
    enc_w,
    enc_m,
    proc_halo,
    proc_w,
    proc_m,
    far_e,
    gath,
    c_out,
    c_in,
    dec_out,
    dec_in,
    dec_g,
    dec_e,
    dec_m,
    grid_lat,
    lat,
    base,
    agg,
    msg,
    w_sem,
    tab_ss,
    tab_rs,
    far_ss,
    far_rs,
    halo_ss,
    halo_rs,
    g_ss,
    g_rs,
    p_ss,
    p_rs,
    y_ss,
    y_rs,
    d_ss,
    d_rs,
):
    nzx = nr // 2
    r = lax.axis_index("row")
    c = lax.axis_index("col")
    core = lax.rem(r, 2)
    zx = r // 2
    up, down = lax.rem(r + 1, nr), lax.rem(r + nr - 1, nr)
    right, left = lax.rem(c + 1, nc), lax.rem(c + nc - 1, nc)
    rows_of = {-1: down, 0: r, 1: up}
    cols_of = {-1: left, 0: c, 1: right}
    partner = r + 1 - 2 * core

    def target(b):
        return (rows_of[b // 3 - 1], cols_of[b % 3 - 1])

    def peer(d):
        return (lax.rem(zx + d, nzx) * 2 + core, c)

    def mate(i):
        return (r, lax.rem(c + nc - i, nc))

    others = [b for b in range(9) if b != 4]
    first_core = core == 0
    x_row = r - 1 + 2 * core
    x_row = lax.rem(x_row + nr, nr)

    barrier = pltpu.get_barrier_semaphore()
    greeted = [target(b) for b in others] + [peer(d) for d in range(1, nzx)] + [mate(2)]
    for device in greeted:
        pl.semaphore_signal(barrier, inc=1, device_id=device, device_id_type=MESH)

    weight_copies = []
    for i in range(4):
        group = []
        for j, (source, place) in enumerate(
            (
                (edge_first_any, ef),
                (edge_second_any, es),
                (node_first_any, nf),
                (node_second_any, ns),
            )
        ):
            copy = pltpu.make_async_copy(source.at[i], place.at[i], w_sem.at[i, j])
            copy.start()
            group.append(copy)
        weight_copies.append(group)
        if i == 0:
            mesh_copies = [pltpu.make_async_copy(mesh_init, mesh_own, w_sem.at[4, 0])]
            mesh_copies[0].start()
    out_copy = pltpu.make_async_copy(out_weight, out_own, w_sem.at[4, 1])
    out_copy.start()

    for b in range(9):
        tab_out[b, 0:1, :] = enc_send[b]
        tab_out[b, 1:2, :] = proc_send[b, :, 0:128]
        tab_out[b, 2:3, :] = proc_send[b, :, 128:256]
        tab_out[b, 3:8, :] = jnp.zeros((5, 128), I32)
    tab_in[0] = tab_out[4]

    hidden = silu(
        lax.dot_general(
            grid_in[...], embed_first[...], (((0,), (0,)), ((), ())), preferred_element_type=F32
        )
    )
    latent = layer_norm(dot(hidden, embed_second[...]), embed_gain[...]).astype(BF)
    grid_lat[...] = latent
    weight_copies[0][0].wait()
    enc_halo[0, 0:G, :] = dot(latent, ef[0, 0]).astype(BF)

    pl.semaphore_wait(barrier, len(greeted))

    toward_partner = 4 + 3 * (1 - 2 * core)
    toward_x = 4 - 3 * (1 - 2 * core)
    tab_copies = []
    for place, block, device in (
        (1, toward_partner, (partner, c)),
        (2, 3, (r, left)),
        (3, 5, (r, right)),
        (4, toward_x, (x_row, c)),
        (5, toward_partner - 1, (partner, left)),
        (6, toward_partner + 1, (partner, right)),
        (7, toward_x - 1, (x_row, left)),
        (8, toward_x + 1, (x_row, right)),
    ):
        copy = pltpu.make_async_remote_copy(
            tab_out.at[block], tab_in.at[place], tab_ss.at[place], tab_rs.at[place],
            device_id=device, device_id_type=MESH,
        )
        copy.start()
        tab_copies.append(copy)

    def send(step, halo, src, dst, first, count, piece, device, started):
        span = pl.ds(first, count)
        copy = pltpu.make_async_remote_copy(
            halo.at[src, span], halo.at[dst, span],
            halo_ss.at[step, dst, piece], halo_rs.at[step, dst, piece],
            device_id=device, device_id_type=MESH,
        )
        copy.start()
        started.append(copy)

    def arrived(step, halo, place, first, count, piece):
        rows = halo.at[place, pl.ds(first, count)]
        pltpu.make_async_copy(rows, rows, halo_rs.at[step, place, piece]).wait()

    def messages(halo, w, size, i, places, msg, extra=None):
        hidden = [silu(dot(w[k], halo[k])) for k in places]
        if extra is not None:
            hidden.append(silu(extra))
        y = dot(jnp.concatenate(hidden, axis=0), es[i])
        first = places[0] * size
        msg[first : first + y.shape[0], :] = layer_norm(y, edge_gain[i : i + 1, :]).astype(BF)

    def node_update(i, own, summed, start):
        node = start + dot(summed.astype(BF), nf[i, 1])
        update = layer_norm(dot(silu(node), ns[i]), node_gain[i : i + 1, :])
        return (own.astype(F32) + update).astype(BF)

    def blocks_at(place):
        return ((4, 4), (1, 7), (3, 3), (5, 5), (7, 1), (0, 6), (2, 8), (6, 0), (8, 2))[place]

    def pick(place, take):
        one, two = blocks_at(place)
        return take(one) if one == two else jnp.where(first_core, take(one), take(two))

    started = []
    send(0, enc_halo, 0, 3, 0, G, 0, (r, right), started)
    send(0, enc_halo, 0, 2, 0, G, 0, (r, left), started)
    send(0, enc_halo, 0, 8, 0, G, 0, (x_row, right), started)
    send(0, enc_halo, 0, 7, 0, G, 0, (x_row, left), started)
    send(0, enc_halo, 0, 4, 0, G, 0, (x_row, c), started)
    send(0, enc_halo, 0, 1, 0, G, 0, (partner, c), started)

    for copy in mesh_copies:
        copy.wait()
    receiver_part = dot(mesh_own[...], ef[0, 1]).astype(BF)
    for k in range(9):
        enc_halo[k, G : G + N, :] = receiver_part

    slot_pad[...] = jnp.full((1, EMP), -1, I32)
    recv_pad[...] = jnp.zeros((1, EMP), I32)
    slot_pad[0:1, 0:EM] = proc_slot[...]
    recv_pad[0:1, 0:EM] = proc_recv[...]
    slot_2d[...] = jnp.full((16, 128), -1, I32)
    chunks = EMP // 128
    for i in range(chunks):
        slot_2d[i : i + 1, :] = slot_pad[0:1, i * 128 : (i + 1) * 128]
    is_far = slot_2d[...] >= FIRST_FAR
    far_ones = ones_where(is_far)
    within = dot(far_ones, ones_where(iota((128, 128), 0) <= iota((128, 128), 1)))
    above = dot(ones_where(iota((16, 16), 1) < iota((16, 16), 0)), far_ones)
    rank = within + jnp.sum(above, axis=1, keepdims=True) - 1.0
    rank = jnp.where(is_far, rank.astype(I32), -1)
    picks = jnp.concatenate(
        [ones_where(rank[i : i + 1, :] == iota((FAR, 128), 0)) for i in range(chunks)], axis=1
    )
    node = jnp.maximum(slot_pad[...] - FIRST_FAR, 0)
    row_id = iota((8, EMP), 0)
    values = jnp.where(
        row_id == 0,
        node >> 6,
        jnp.where(
            row_id == 1,
            node & 63,
            jnp.where(row_id == 2, recv_pad[...] >> 6, jnp.where(row_id == 3, recv_pad[...] & 63, 0)),
        ),
    )
    values = values.astype(F32).astype(BF)
    far_cols = dot_nt(picks, values)
    far_rows = dot_nt(values, picks)
    far_node = (far_cols[:, 0:1] * 64.0 + far_cols[:, 1:2]).astype(I32)
    far_out[...] = jnp.broadcast_to(far_node, (FAR, 128))
    far_in[0] = jnp.broadcast_to(far_node, (FAR, 128))
    far_copies = []
    for i in range(1, nc):
        copy = pltpu.make_async_remote_copy(
            far_out, far_in.at[nc - i], far_ss.at[nc - i], far_rs.at[nc - i],
            device_id=mate(i), device_id_type=MESH,
        )
        copy.start()
        far_copies.append(copy)
    far_recv_col = (far_cols[:, 2:3] * 64.0 + far_cols[:, 3:4]).astype(I32)
    far_recv_row = (far_rows[2:3, :] * 64.0 + far_rows[3:4, :]).astype(I32)
    far_e[...] = ones_where(far_recv_col == iota((FAR, N), 1))
    proc_m[:, 9 * CM :] = ones_where(far_recv_row == iota((N, FAR), 0))

    enc_rows, enc_cols = slot_receivers(enc_slot[...], enc_recv[...], 16)
    for copy in tab_copies:
        copy.wait_recv()
    tab_t[0:72, :] = tab_in[...].reshape(72, 128).astype(F32)
    tab_t[72:128, :] = jnp.zeros((56, 128), F32)
    tabs = jnp.transpose(tab_t[...]).astype(I32)
    for k in range(9):
        at = iota((CE, G + N), 1)
        receiver = pick(k, lambda b: enc_cols[:, b : b + 1])
        receiver = jnp.where(receiver < 0, -1, receiver + G)
        enc_w[k] = ones_where((at == tabs[:, 8 * k : 8 * k + 1]) | (at == receiver))
        receiver = pick(k, lambda b: enc_rows[b : b + 1, :])
        enc_m[:, k * CE : (k + 1) * CE] = ones_where(receiver == iota((N, CE), 0))

    weight_copies[0][1].wait()
    messages(enc_halo, enc_w, CE, 0, (0,), msg)
    arrived(0, enc_halo, 2, 0, G, 0)
    send(0, enc_halo, 2, 5, 0, G, 0, (partner, c), started)
    arrived(0, enc_halo, 3, 0, G, 0)
    send(0, enc_halo, 3, 6, 0, G, 0, (partner, c), started)
    weight_copies[0][2].wait()
    weight_copies[0][3].wait()
    base[...] = dot(mesh_own[...], nf[0, 0])
    arrived(0, enc_halo, 1, 0, G, 0)
    messages(enc_halo, enc_w, CE, 0, (1, 2, 3), msg)

    proc_rows, proc_cols = slot_receivers(slot_pad[...], recv_pad[...], 24)
    for k in range(9):
        at = iota((128, 2 * N), 1)
        for half in range(2):
            receiver = pick(k, lambda b: proc_cols[:, 2 * b + half : 2 * b + half + 1])
            receiver = jnp.where(receiver < 0, -1, receiver + N)
            sender = tabs[:, 8 * k + 1 + half : 8 * k + 2 + half]
            span = slice(half * 128, (half + 1) * 128)
            proc_w[k, span, :] = ones_where((at == sender) | (at == receiver))
            receiver = pick(k, lambda b: proc_rows[2 * b + half : 2 * b + half + 1, :])
            first = k * CM + half * 128
            proc_m[:, first : first + 128] = ones_where(receiver == iota((N, 128), 0))

    dec_rows, dec_cols = slot_receivers(dec_slot[...], dec_recv[...], 16)
    for h in range(5):
        span = slice(h * 128, (h + 1) * 128)
        dec_e[span, :] = ones_where(dec_cols[:, h : h + 1] == iota((128, G), 1))
        dec_m[:, span] = ones_where(dec_rows[h : h + 1, :] == iota((G, 128), 0))
    tab_t[...] = jnp.zeros((128, 128), F32)
    for b in range(9):
        tab_t[b : b + 1, 0:CD] = dec_send[b].astype(F32)
    dec_tabs = jnp.transpose(tab_t[...]).astype(I32)
    for b in range(9):
        dec_g[b * CD : (b + 1) * CD, :] = ones_where(dec_tabs[0:CD, b : b + 1] == iota((CD, N), 1))
    dec_in[9 * CD : 640, :] = jnp.zeros((64, L), BF)

    for k in (4, 5, 6):
        arrived(0, enc_halo, k, 0, G, 0)
    messages(enc_halo, enc_w, CE, 0, (4, 5, 6), msg)
    agg[...] = dot(enc_m[:, 0 : 7 * CE], msg[0 : 7 * CE, :])
    for k in (7, 8):
        arrived(0, enc_halo, k, 0, G, 0)
    messages(enc_halo, enc_w, CE, 0, (7, 8), msg)
    summed = agg[...] + dot(enc_m[:, 7 * CE : 9 * CE], msg[7 * CE : 9 * CE, :])
    lat[...] = node_update(0, mesh_own[...], summed, base[...])
    for copy in started + tab_copies + far_copies:
        copy.wait_send()

    for s in range(2):
        i = s + 1
        halo = proc_halo.at[s]
        for copy in weight_copies[i]:
            copy.wait()
        own = lat[...]
        sent = dot(own, ef[i, 0]).astype(BF)
        halo[0, 0:N, :] = sent
        place = pl.multiple_of((core * nzx + zx) * CO, CO)
        gath[s, pl.ds(place, CO), :] = sent[0:CO, :]
        peer_copies = []
        for d in range(1, nzx):
            copy = pltpu.make_async_remote_copy(
                gath.at[s, pl.ds(place, CO)], gath.at[s, pl.ds(place, CO)],
                g_ss.at[s, d], g_rs.at[s, d], device_id=peer(d), device_id_type=MESH,
            )
            copy.start()
            peer_copies.append(copy)
        started = []
        for piece in range(4):
            send(i, halo, 0, 3, piece * CH, CH, piece, (r, right), started)
            send(i, halo, 0, 2, piece * CH, CH, piece, (r, left), started)
            if piece == 0:
                send(i, halo, 0, 4, 3 * CH, CH, 3, (x_row, c), started)
                send(i, halo, 0, 4, 0, 3 * CH, 0, (x_row, c), started)
                send(i, halo, 0, 1, 0, N, 0, (partner, c), started)
        receiver_part = dot(own, ef[i, 1]).astype(BF)
        for k in range(9):
            halo[k, N : 2 * N, :] = receiver_part
        base[...] = dot(own, nf[i, 0])
        arrived(i, halo, 1, 0, N, 0)
        messages(halo, proc_w, CM, i, (0, 1), msg)
        for piece in range(3):
            arrived(i, halo, 2, piece * CH, CH, piece)
            send(i, halo, 2, 7, piece * CH, CH, piece, (x_row, c), started)
            arrived(i, halo, 3, piece * CH, CH, piece)
            send(i, halo, 3, 8, piece * CH, CH, piece, (x_row, c), started)
            if piece == 0:
                arrived(i, halo, 4, 3 * CH, CH, 3)
                send(i, halo, 4, 8, 3 * CH, CH, 3, (r, right), started)
                send(i, halo, 4, 7, 3 * CH, CH, 3, (r, left), started)
        arrived(i, halo, 2, 3 * CH, CH, 3)
        send(i, halo, 2, 5, 0, N, 0, (partner, c), started)
        arrived(i, halo, 3, 3 * CH, CH, 3)
        send(i, halo, 3, 6, 0, N, 0, (partner, c), started)
        for copy in peer_copies:
            copy.wait_recv()
        mine = pl.ds(pl.multiple_of(core * (nzx * CO), CO), nzx * CO)
        to_partner = pltpu.make_async_remote_copy(
            gath.at[s, mine], gath.at[s, mine], p_ss.at[s], p_rs.at[s],
            device_id=(partner, c), device_id_type=MESH,
        )
        to_partner.start()
        messages(halo, proc_w, CM, i, (2, 3), msg)

        to_partner.wait_recv()
        if s == 0:
            for copy in far_copies:
                copy.wait_recv()
        found = []
        for q in range(nc):
            number = far_in[q]
            device = number // CO
            band = device // nc
            index = (band % 2) * (nzx * CO) + (band // 2) * CO + number % CO
            index = jnp.where(device % nc == c, index, -1)
            found.append(
                jnp.concatenate(
                    [ones_where(index == iota((FAR, 128), 1) + 128 * t) for t in range(max(1, nr * CO // 128))],
                    axis=1,
                )
            )
        chosen = dot(jnp.concatenate(found, axis=0), gath[s]).astype(BF)
        c_out[s] = chosen
        mate_copies = []
        for q in range(1, nc):
            copy = pltpu.make_async_remote_copy(
                c_out.at[s, pl.ds(q * FAR, FAR)], c_in.at[s, q], y_ss.at[s, q], y_rs.at[s, q],
                device_id=mate(q), device_id_type=MESH,
            )
            copy.start()
            mate_copies.append(copy)

        arrived(i, halo, 4, 0, 3 * CH, 0)
        for k in (5, 6):
            arrived(i, halo, k, 0, N, 0)
        messages(halo, proc_w, CM, i, (4, 5, 6), msg)
        agg[...] = dot(proc_m[:, 0 : 7 * CM], msg[0 : 7 * CM, :])
        pre = c_out[s, 0:FAR, :].astype(F32) + dot(far_e[...], halo[0, N : 2 * N, :])
        for copy in mate_copies:
            copy.wait_recv()
        for q in range(1, nc):
            pre = pre + c_in[s, q].astype(F32)
        for k in (7, 8):
            for piece in range(4):
                arrived(i, halo, k, piece * CH, CH, piece)
        messages(halo, proc_w, CM, i, (7, 8), msg, pre)
        summed = agg[...] + dot(proc_m[:, 7 * CM :], msg[7 * CM :, :])
        lat[...] = node_update(i, own, summed, base[...])
        for copy in started + peer_copies + mate_copies + [to_partner]:
            copy.wait_send()

    for copy in weight_copies[3]:
        copy.wait()
    sent = dot(lat[...], ef[3, 0]).astype(BF)
    dec_out[...] = dot(dec_g[...], sent).astype(BF)
    dec_copies = []
    for b in others:
        span = pl.ds(b * CD, CD)
        copy = pltpu.make_async_remote_copy(
            dec_out.at[span], dec_in.at[span], d_ss.at[b], d_rs.at[b],
            device_id=target(b), device_id_type=MESH,
        )
        copy.start()
        dec_copies.append(copy)
    dec_in[4 * CD : 5 * CD, :] = dec_out[4 * CD : 5 * CD, :]
    own = grid_lat[...]
    receiver_part = dot(own, ef[3, 1]).astype(BF)
    near = dot(dec_e[...], receiver_part)
    start = dot(own, nf[3, 0])
    for copy in dec_copies:
        copy.wait_recv()
    pre = dec_in[...].astype(F32) + near
    y = dot(silu(pre), es[3])
    message = layer_norm(y, edge_gain[3:4, :]).astype(BF)
    out_copy.wait()
    final = node_update(3, own, dot(dec_m[...], message), start)
    out[...] = grid_in[...].astype(F32) + dot_nt(out_own[...], final)
    for copy in dec_copies:
        copy.wait_send()


def on_device(nr, nc, *args):
    vmem = pl.BlockSpec(memory_space=pltpu.VMEM)
    hbm = pl.BlockSpec(memory_space=pl.ANY)
    in_specs = [vmem] * 21
    for at in (1, 5, 6, 8, 9, 11):
        in_specs[at] = hbm
    args = list(args)
    args[4] = args[4].reshape(1, L)
    args[0] = args[0].T
    args[11] = args[11].T
    for at in (12, 15, 18):
        args[at] = jnp.transpose(args[at], (1, 0, 2))
    dma = pltpu.SemaphoreType.DMA
    nzx = nr // 2
    prediction = pl.pallas_call(
        functools.partial(body, nr, nc),
        out_shape=jax.ShapeDtypeStruct((CIN, G), F32),
        in_specs=in_specs,
        out_specs=vmem,
        scratch_shapes=[
            pltpu.VMEM((4, 2, L, L), BF),
            pltpu.VMEM((4, L, L), BF),
            pltpu.VMEM((4, 2, L, L), BF),
            pltpu.VMEM((4, L, L), BF),
            pltpu.VMEM((N, L), BF),
            pltpu.VMEM((CIN, L), BF),
            pltpu.VMEM((9, 8, 128), I32),
            pltpu.VMEM((9, 8, 128), I32),
            pltpu.VMEM((128, 128), F32),
            pltpu.VMEM((FAR, 128), I32),
            pltpu.VMEM((nc, FAR, 128), I32),
            pltpu.VMEM((1, EMP), I32),
            pltpu.VMEM((1, EMP), I32),
            pltpu.VMEM((16, 128), I32),
            pltpu.VMEM((9, G + N, L), BF),
            pltpu.VMEM((9, CE, G + N), BF),
            pltpu.VMEM((N, 9 * CE), BF),
            pltpu.VMEM((2, 9, 2 * N, L), BF),
            pltpu.VMEM((9, CM, 2 * N), BF),
            pltpu.VMEM((N, 9 * CM + FAR), BF),
            pltpu.VMEM((FAR, N), BF),
            pltpu.VMEM((2, nr * CO, L), BF),
            pltpu.VMEM((2, nc * FAR, L), BF),
            pltpu.VMEM((2, nc, FAR, L), BF),
            pltpu.VMEM((9 * CD, L), BF),
            pltpu.VMEM((640, L), BF),
            pltpu.VMEM((9 * CD, N), BF),
            pltpu.VMEM((640, G), BF),
            pltpu.VMEM((G, 640), BF),
            pltpu.VMEM((G, L), BF),
            pltpu.VMEM((N, L), BF),
            pltpu.VMEM((N, L), F32),
            pltpu.VMEM((N, L), F32),
            pltpu.VMEM((9 * CM + FAR, L), BF),
            dma((5, 4)),
            dma((9,)),
            dma((9,)),
            dma((nc,)),
            dma((nc,)),
            dma((3, 9, 4)),
            dma((3, 9, 4)),
            dma((2, nzx)),
            dma((2, nzx)),
            dma((2,)),
            dma((2,)),
            dma((2, nc)),
            dma((2, nc)),
            dma((9,)),
            dma((9,)),
        ],
        compiler_params=pltpu.CompilerParams(
            collective_id=0, has_side_effects=True, vmem_limit_bytes=60 * 1024 * 1024
        ),
    )(*args)
    return prediction.T


def solution(mesh):
    both = ("row", "col")
    placed = (
        (P(both, None),) * 2
        + (P(),) * 10
        + (P(both, None, None), P(both, None), P(both, None)) * 3
    )
    return jax.shard_map(
        functools.partial(on_device, mesh.shape["row"], mesh.shape["col"]),
        mesh=mesh,
        in_specs=placed,
        out_specs=P(both, None),
        check_vma=False,
    )
```

```python
import functools

import jax
import jax.numpy as jnp
from jax import lax
from jax.experimental import pallas as pl
from jax.experimental.pallas import tpu as pltpu
from jax.sharding import PartitionSpec as P

BF = jnp.bfloat16
F32 = jnp.float32
I32 = jnp.int32
MESH = pl.DeviceIdType.MESH

L = 512
CIN = 227
G = 128
N = 320
CO = 16
FAR = 64
CE, CM, CD = 128, 256, 64
EE, EM, ED = 768, 1600, 384
EMP = 1664
FIRST_FAR = 9 * CM
EPSILON = 1e-05

PIECES = ((0, 64), (64, 64), (128, 128), (256, 64))
LAST = len(PIECES) - 1
CH = 80
GRID_PIECES = ((0, 64), (64, 64))


def dot(a, b):
    return jnp.dot(a, b, preferred_element_type=F32)


def dot_nt(a, b):
    return lax.dot_general(a, b, (((1,), (1,)), ((), ())), preferred_element_type=F32)


def iota(shape, dim):
    return lax.broadcasted_iota(I32, shape, dim)


def ones_where(cond):
    return jnp.where(cond, 1.0, 0.0).astype(BF)


def silu(v):
    u = 0.5 * v
    return (u + u * jnp.tanh(u)).astype(BF)


def layer_norm(y, gain):
    average = jnp.mean(y, axis=-1, keepdims=True)
    centered = y - average
    spread = jnp.mean(centered * centered, axis=-1, keepdims=True)
    return centered * lax.rsqrt(spread + EPSILON) * gain


def slot_receivers(slot, recv, high):
    edges = slot.shape[1]
    at_high = (slot >> 7) == iota((high, edges), 0)
    code = recv + 1
    first = jnp.where(at_high, (code >> 6).astype(F32), 0.0).astype(BF)
    second = jnp.where(at_high, (code & 63).astype(F32), 0.0).astype(BF)
    at_low = ones_where((slot & 127) == iota((128, edges), 0))
    rows = dot_nt(first, at_low) * 64.0 + dot_nt(second, at_low) - 1.0
    cols = dot_nt(at_low, first) * 64.0 + dot_nt(at_low, second) - 1.0
    return rows.astype(I32), cols.astype(I32)


def body(
    nr,
    nc,
    grid_in_any,
    mesh_init,
    embed_first_any,
    embed_second_any,
    embed_gain_any,
    edge_first_any,
    edge_second_any,
    edge_gain_any,
    node_first_any,
    node_second_any,
    node_gain_any,
    out_weight,
    enc_send_any,
    enc_slot_any,
    enc_recv_any,
    proc_send_any,
    proc_slot_any,
    proc_recv_any,
    dec_send_any,
    dec_slot_any,
    dec_recv_any,
    out,
    enc_send,
    proc_send,
    grid_in,
    embed_first,
    embed_second,
    embed_gain,
    proc_slot,
    proc_recv,
    enc_slot,
    enc_recv,
    edge_gain,
    node_gain,
    dec_send,
    dec_slot,
    dec_recv,
    ef,
    es,
    nf,
    ns,
    mesh_own,
    out_own,
    tab_out,
    tab_in,
    tab_side,
    tab_t,
    tab_cols,
    far_out,
    far_in,
    far_pick,
    slot_pad,
    recv_pad,
    slot_2d,
    enc_halo,
    enc_w,
    enc_m,
    proc_halo,
    proc_w,
    proc_m,
    far_e,
    gath,
    c_out,
    c_in,
    dec_out,
    dec_in,
    dec_g,
    dec_e,
    dec_m,
    grid_lat,
    lat,
    base,
    agg,
    msg,
    w_sem,
    in_sem,
    tab_ss,
    tab_rs,
    far_ss,
    far_rs,
    halo_ss,
    halo_rs,
    g_ss,
    g_rs,
    p_ss,
    p_rs,
    y_ss,
    y_rs,
    d_ss,
    d_rs,
):
    nzx = nr // 2
    r = lax.axis_index("row")
    c = lax.axis_index("col")
    core = lax.rem(r, 2)
    zx = r // 2
    up, down = lax.rem(r + 1, nr), lax.rem(r + nr - 1, nr)
    right, left = lax.rem(c + 1, nc), lax.rem(c + nc - 1, nc)
    rows_of = {-1: down, 0: r, 1: up}
    cols_of = {-1: left, 0: c, 1: right}
    partner = r + 1 - 2 * core

    def target(b):
        return (rows_of[b // 3 - 1], cols_of[b % 3 - 1])

    def peer(d):
        return (lax.rem(zx + d, nzx) * 2 + core, c)

    def mate(i):
        return (r, lax.rem(c + nc - i, nc))

    others = [b for b in range(9) if b != 4]
    first_core = core == 0
    x_row = r - 1 + 2 * core
    x_row = lax.rem(x_row + nr, nr)

    barrier = pltpu.get_barrier_semaphore()
    greeted = [(x_row, c)] + [peer(d) for d in range(1, nzx)]
    greeted += [mate(2), (r, left), (r, right), (partner, c)]
    for device in greeted:
        pl.semaphore_signal(barrier, inc=1, device_id=device, device_id_type=MESH)

    loads = []
    for at, (source, place) in enumerate(
        (
            (enc_send_any, enc_send),
            (proc_send_any, proc_send),
            (grid_in_any, grid_in),
            (embed_first_any, embed_first),
            (embed_second_any, embed_second),
            (embed_gain_any, embed_gain),
            (proc_slot_any, proc_slot),
            (proc_recv_any, proc_recv),
            (enc_slot_any, enc_slot),
            (enc_recv_any, enc_recv),
            (edge_gain_any, edge_gain),
            (node_gain_any, node_gain),
            (dec_send_any, dec_send),
            (dec_slot_any, dec_slot),
            (dec_recv_any, dec_recv),
        )
    ):
        copy = pltpu.make_async_copy(source, place, in_sem.at[at])
        copy.start()
        loads.append(copy)

    weight_copies = []
    for i in range(4):
        group = []
        for j, (source, place) in enumerate(
            (
                (edge_first_any, ef),
                (edge_second_any, es),
                (node_first_any, nf),
                (node_second_any, ns),
            )
        ):
            copy = pltpu.make_async_copy(source.at[i], place.at[i], w_sem.at[i, j])
            group.append(copy)
            if i == 0:
                copy.start()
        weight_copies.append(group)
        if i == 0:
            mesh_copies = [pltpu.make_async_copy(mesh_init, mesh_own, w_sem.at[4, 0])]
            mesh_copies[0].start()
    out_copy = pltpu.make_async_copy(out_weight, out_own, w_sem.at[4, 1])

    for copy in loads:
        copy.wait()

    toward_partner = 4 + 3 * (1 - 2 * core)
    toward_x = 4 - 3 * (1 - 2 * core)
    for at, b in enumerate(
        (4, toward_partner, toward_x)
        + (5, toward_partner + 1, toward_x + 1)
        + (3, toward_partner - 1, toward_x - 1)
    ):
        tab_out[at, 0:1, :] = enc_send[b]
        tab_out[at, 1:2, :] = proc_send[b, :, 0:128]
        tab_out[at, 2:3, :] = proc_send[b, :, 128:256]
        tab_out[at, 3:8, :] = jnp.zeros((5, 128), I32)

    hidden = silu(
        lax.dot_general(
            grid_in[...], embed_first[...], (((0,), (0,)), ((), ())), preferred_element_type=F32
        )
    )
    latent = layer_norm(dot(hidden, embed_second[...]), embed_gain[...]).astype(BF)
    grid_lat[...] = latent
    weight_copies[0][0].wait()
    enc_halo[0, 0:G, :] = dot(latent, ef[0, 0]).astype(BF)

    pl.semaphore_wait(barrier, len(greeted))

    tab_copies = []

    def send_tab(source, place, at, device):
        copy = pltpu.make_async_remote_copy(
            source, place, tab_ss.at[at], tab_rs.at[at], device_id=device, device_id_type=MESH
        )
        copy.start()
        tab_copies.append(copy)

    def send(step, halo, src, dst, first, count, piece, device, started):
        span = pl.ds(first, count)
        copy = pltpu.make_async_remote_copy(
            halo.at[src, span], halo.at[dst, span],
            halo_ss.at[step, dst, piece], halo_rs.at[step, dst, piece],
            device_id=device, device_id_type=MESH,
        )
        copy.start()
        started.append(copy)

    def arrived(step, halo, place, first, count, piece):
        rows = halo.at[place, pl.ds(first, count)]
        pltpu.make_async_copy(rows, rows, halo_rs.at[step, place, piece]).wait()

    def messages(halo, w, size, i, places, msg, extra=None):
        hidden = [silu(dot(w[k], halo[k])) for k in places]
        if extra is not None:
            hidden.append(silu(extra))
        y = dot(jnp.concatenate(hidden, axis=0), es[i])
        first = places[0] * size
        msg[first : first + y.shape[0], :] = layer_norm(y, edge_gain[i : i + 1, :]).astype(BF)

    def node_update(i, own, summed, start):
        node = start + dot(summed.astype(BF), nf[i, 1])
        update = layer_norm(dot(silu(node), ns[i]), node_gain[i : i + 1, :])
        return (own.astype(F32) + update).astype(BF)

    def begin_step(i, first, count, latents, started, pushes):
        s = i - 1
        halo = proc_halo.at[s]
        sent = dot(latents, ef[i, 0]).astype(BF)
        halo[0, first : first + count, :] = sent
        if first == 0:
            place = pl.ds(pl.multiple_of((core * nzx + zx) * CO, CO), CO)
            gath[s, place, :] = sent[0:CO, :]
            for d in range(1, nzx):
                copy = pltpu.make_async_remote_copy(
                    gath.at[s, place], gath.at[s, place],
                    g_ss.at[s, d], g_rs.at[s, d], device_id=peer(d), device_id_type=MESH,
                )
                copy.start()
                pushes.append(copy)
            pieces = (0,)
        else:
            send(i, halo, 0, 4, 3 * CH, CH, 3, (x_row, c), started)
            send(i, halo, 0, 4, 0, 3 * CH, 0, (x_row, c), started)
            send(i, halo, 0, 1, 0, N, 0, (partner, c), started)
            pieces = (1, 2, 3)
        for piece in pieces:
            send(i, halo, 0, 3, piece * CH, CH, piece, (r, right), started)
            send(i, halo, 0, 2, piece * CH, CH, piece, (r, left), started)

    def finish_step(i, own, m, first, last):
        started, pushes = [], []
        if i < 2:
            for copy in weight_copies[i + 1]:
                copy.wait()
        for at, count in ((0, CH), (CH, N - CH)):
            part = slice(at, at + count)
            summed = agg[part, :] + dot(m[part, first:last], msg[first:last, :])
            latents = node_update(i, own[part, :], summed, base[part, :])
            lat[part, :] = latents
            if i < 2:
                begin_step(i + 1, at, count, latents, started, pushes)
        return started, pushes

    def blocks_at(place):
        return ((4, 4), (1, 7), (3, 3), (5, 5), (7, 1), (0, 6), (2, 8), (6, 0), (8, 2))[place]

    def pick(place, take):
        one, two = blocks_at(place)
        return take(one) if one == two else jnp.where(first_core, take(one), take(two))

    started = []
    send_tab(tab_out.at[pl.ds(3, 3)], tab_side.at[1], 3, (r, right))
    send_tab(tab_out.at[pl.ds(6, 3)], tab_side.at[0], 2, (r, left))
    send_tab(tab_out.at[1], tab_in.at[1], 1, (partner, c))
    send_tab(tab_out.at[2], tab_in.at[4], 4, (x_row, c))
    for piece, (first, count) in enumerate(GRID_PIECES):
        send(0, enc_halo, 0, 3, first, count, piece, (r, right), started)
        send(0, enc_halo, 0, 2, first, count, piece, (r, left), started)
        if piece == 0:
            send(0, enc_halo, 0, 4, 0, G, 0, (x_row, c), started)
            send(0, enc_halo, 0, 1, 0, G, 0, (partner, c), started)

    for copy in mesh_copies:
        copy.wait()
    receiver_part = dot(mesh_own[...], ef[0, 1]).astype(BF)
    for k in range(9):
        enc_halo[k, G : G + N, :] = receiver_part

    slot_pad[...] = jnp.full((1, EMP), -1, I32)
    recv_pad[...] = jnp.zeros((1, EMP), I32)
    slot_pad[0:1, 0:EM] = proc_slot[...]
    recv_pad[0:1, 0:EM] = proc_recv[...]
    slot_2d[...] = jnp.full((16, 128), -1, I32)
    chunks = EMP // 128
    for i in range(chunks):
        slot_2d[i : i + 1, :] = slot_pad[0:1, i * 128 : (i + 1) * 128]
    is_far = slot_2d[...] >= FIRST_FAR
    far_ones = ones_where(is_far)
    within = dot(far_ones, ones_where(iota((128, 128), 0) <= iota((128, 128), 1)))
    above = dot(ones_where(iota((16, 16), 1) < iota((16, 16), 0)), far_ones)
    rank = within + jnp.sum(above, axis=1, keepdims=True) - 1.0
    rank = jnp.where(is_far, rank.astype(I32), -1)
    picks = jnp.concatenate(
        [ones_where(rank[i : i + 1, :] == iota((FAR, 128), 0)) for i in range(chunks)], axis=1
    )
    node = jnp.maximum(slot_pad[...] - FIRST_FAR, 0)
    row_id = iota((8, EMP), 0)
    values = jnp.where(
        row_id == 0,
        node >> 6,
        jnp.where(
            row_id == 1,
            node & 63,
            jnp.where(row_id == 2, recv_pad[...] >> 6, jnp.where(row_id == 3, recv_pad[...] & 63, 0)),
        ),
    )
    values = values.astype(F32).astype(BF)
    far_cols = dot_nt(picks, values)
    far_rows = dot_nt(values, picks)
    far_node = (far_cols[:, 0:1] * 64.0 + far_cols[:, 1:2]).astype(I32)
    far_out[...] = jnp.broadcast_to(far_node, (FAR, 128))
    far_in[0] = jnp.broadcast_to(far_node, (FAR, 128))
    far_copies = []
    for i in range(1, nc):
        copy = pltpu.make_async_remote_copy(
            far_out, far_in.at[nc - i], far_ss.at[nc - i], far_rs.at[nc - i],
            device_id=mate(i), device_id_type=MESH,
        )
        copy.start()
        far_copies.append(copy)
    far_recv_col = (far_cols[:, 2:3] * 64.0 + far_cols[:, 3:4]).astype(I32)
    far_recv_row = (far_rows[2:3, :] * 64.0 + far_rows[3:4, :]).astype(I32)
    far_e[...] = ones_where(far_recv_col == iota((FAR, N), 1))
    proc_m[:, 9 * CM :] = ones_where(far_recv_row == iota((N, FAR), 0))

    enc_rows, enc_cols = slot_receivers(enc_slot[...], enc_recv[...], 16)
    for k in range(9):
        receiver = pick(k, lambda b: enc_rows[b : b + 1, :])
        enc_m[:, k * CE : (k + 1) * CE] = ones_where(receiver == iota((N, CE), 0))

    def tables(places, at):
        first, count = places[0], len(places)
        tab_t[0 : 8 * count, :] = tab_in[first : first + count].reshape(8 * count, 128).astype(F32)
        tab_t[8 * count :, :] = jnp.zeros((128 - 8 * count, 128), F32)
        tab_cols[at] = jnp.transpose(tab_t[...]).astype(I32)

    def enc_matrices(places, at):
        for k in places:
            here = iota((CE, G + N), 1)
            receiver = pick(k, lambda b: enc_cols[:, b : b + 1])
            receiver = jnp.where(receiver < 0, -1, receiver + G)
            column = 8 * (k - places[0])
            sender = tab_cols[at, :, column : column + 1]
            enc_w[k] = ones_where((here == sender) | (here == receiver))

    def proc_matrices(places, at):
        for k in places:
            here = iota((128, 2 * N), 1)
            for half in range(2):
                receiver = pick(k, lambda b: proc_cols[:, 2 * b + half : 2 * b + half + 1])
                receiver = jnp.where(receiver < 0, -1, receiver + N)
                column = 8 * (k - places[0]) + 1 + half
                sender = tab_cols[at, :, column : column + 1]
                span = slice(half * 128, (half + 1) * 128)
                proc_w[k, span, :] = ones_where((here == sender) | (here == receiver))

    def dec_matrices():
        dec_rows, dec_cols = slot_receivers(dec_slot[...], dec_recv[...], 16)
        for h in range(5):
            span = slice(h * 128, (h + 1) * 128)
            dec_e[span, :] = ones_where(dec_cols[:, h : h + 1] == iota((128, G), 1))
            dec_m[:, span] = ones_where(dec_rows[h : h + 1, :] == iota((G, 128), 0))
        tab_t[...] = jnp.zeros((128, 128), F32)
        for b in range(9):
            tab_t[b : b + 1, 0:CD] = dec_send[b].astype(F32)
        dec_tabs = jnp.transpose(tab_t[...]).astype(I32)
        for b in range(9):
            dec_g[b * CD : (b + 1) * CD, :] = ones_where(dec_tabs[0:CD, b : b + 1] == iota((CD, N), 1))
        dec_in[9 * CD : 640, :] = jnp.zeros((64, L), BF)

    for group in weight_copies[1:]:
        for copy in group:
            copy.start()
    out_copy.start()
    tab_copies[0].wait_recv()
    tab_copies[1].wait_recv()
    send_tab(tab_side.at[0, 1], tab_in.at[5], 5, (partner, c))
    send_tab(tab_side.at[0, 2], tab_in.at[7], 7, (x_row, c))
    send_tab(tab_side.at[1, 1], tab_in.at[6], 6, (partner, c))
    send_tab(tab_side.at[1, 2], tab_in.at[8], 8, (x_row, c))
    tab_in[0] = tab_out[0]
    tab_in[2] = tab_side[0, 0]
    tab_in[3] = tab_side[1, 0]
    for piece, (first, count) in enumerate(GRID_PIECES):
        arrived(0, enc_halo, 2, first, count, piece)
        send(0, enc_halo, 2, 7, first, count, piece, (x_row, c), started)
        arrived(0, enc_halo, 3, first, count, piece)
        send(0, enc_halo, 3, 8, first, count, piece, (x_row, c), started)
    send(0, enc_halo, 2, 5, 0, G, 0, (partner, c), started)
    send(0, enc_halo, 3, 6, 0, G, 0, (partner, c), started)
    tab_copies[2].wait_recv()
    tab_copies[3].wait_recv()
    near = (0, 1, 2, 3, 4)
    tables(near, 0)
    enc_matrices(near, 0)
    for copy in weight_copies[0][1:]:
        copy.wait()
    arrived(0, enc_halo, 1, 0, G, 0)
    arrived(0, enc_halo, 4, 0, G, 0)
    messages(enc_halo, enc_w, CE, 0, near, msg)
    base[...] = dot(mesh_own[...], nf[0, 0])
    for copy in tab_copies[4:]:
        copy.wait_recv()
    diagonal = (5, 6, 7, 8)
    tables(diagonal, 1)
    enc_matrices(diagonal, 1)
    arrived(0, enc_halo, 5, 0, G, 0)
    arrived(0, enc_halo, 6, 0, G, 0)
    messages(enc_halo, enc_w, CE, 0, (5, 6), msg)
    agg[...] = dot(enc_m[:, 0 : 7 * CE], msg[0 : 7 * CE, :])

    proc_rows, proc_cols = slot_receivers(slot_pad[...], recv_pad[...], 24)
    for k in range(9):
        for half in range(2):
            receiver = pick(k, lambda b: proc_rows[2 * b + half : 2 * b + half + 1, :])
            first = k * CM + half * 128
            proc_m[:, first : first + 128] = ones_where(receiver == iota((N, 128), 0))
    proc_matrices(near, 0)
    dec_matrices()
    for copy in far_copies:
        copy.wait_recv()
    found = []
    for q in range(nc):
        number = far_in[q]
        device = number // CO
        band = device // nc
        index = (band % 2) * (nzx * CO) + (band // 2) * CO + number % CO
        index = jnp.where(device % nc == c, index, -1)
        found.append(
            jnp.concatenate(
                [ones_where(index == iota((FAR, 128), 1) + 128 * t) for t in range(max(1, nr * CO // 128))],
                axis=1,
            )
        )
    far_pick[...] = jnp.concatenate(found, axis=0)

    for k in (7, 8):
        for piece, (first, count) in enumerate(GRID_PIECES):
            arrived(0, enc_halo, k, first, count, piece)
    messages(enc_halo, enc_w, CE, 0, (7, 8), msg)
    ahead, pushes = finish_step(0, mesh_own[...], enc_m, 7 * CE, 9 * CE)
    for copy in started + tab_copies + far_copies:
        copy.wait_send()

    for s in range(2):
        i = s + 1
        halo = proc_halo.at[s]
        own = lat[...]
        started, peer_copies = ahead, pushes
        receiver_part = dot(own, ef[i, 1]).astype(BF)
        for k in range(9):
            halo[k, N : 2 * N, :] = receiver_part
        base[...] = dot(own, nf[i, 0])
        arrived(i, halo, 1, 0, N, 0)
        messages(halo, proc_w, CM, i, (0, 1), msg)
        for piece in range(3):
            arrived(i, halo, 2, piece * CH, CH, piece)
            send(i, halo, 2, 7, piece * CH, CH, piece, (x_row, c), started)
            arrived(i, halo, 3, piece * CH, CH, piece)
            send(i, halo, 3, 8, piece * CH, CH, piece, (x_row, c), started)
            if piece == 0:
                arrived(i, halo, 4, 3 * CH, CH, 3)
                send(i, halo, 4, 8, 3 * CH, CH, 3, (r, right), started)
                send(i, halo, 4, 7, 3 * CH, CH, 3, (r, left), started)
        arrived(i, halo, 2, 3 * CH, CH, 3)
        send(i, halo, 2, 5, 0, N, 0, (partner, c), started)
        arrived(i, halo, 3, 3 * CH, CH, 3)
        send(i, halo, 3, 6, 0, N, 0, (partner, c), started)
        for copy in peer_copies:
            copy.wait_recv()
        mine = pl.ds(pl.multiple_of(core * (nzx * CO), CO), nzx * CO)
        to_partner = pltpu.make_async_remote_copy(
            gath.at[s, mine], gath.at[s, mine], p_ss.at[s], p_rs.at[s],
            device_id=(partner, c), device_id_type=MESH,
        )
        to_partner.start()
        to_partner.wait_recv()
        chosen = dot(far_pick[...], gath[s]).astype(BF)
        c_out[s] = chosen
        mate_copies = []
        for q in range(1, nc):
            copy = pltpu.make_async_remote_copy(
                c_out.at[s, pl.ds(q * FAR, FAR)], c_in.at[s, q], y_ss.at[s, q], y_rs.at[s, q],
                device_id=mate(q), device_id_type=MESH,
            )
            copy.start()
            mate_copies.append(copy)

        messages(halo, proc_w, CM, i, (2, 3), msg)
        if s == 0:
            proc_matrices(diagonal, 1)
        arrived(i, halo, 4, 0, 3 * CH, 0)
        for k in (5, 6):
            arrived(i, halo, k, 0, N, 0)
        messages(halo, proc_w, CM, i, (4, 5, 6), msg)
        agg[...] = dot(proc_m[:, 0 : 7 * CM], msg[0 : 7 * CM, :])
        pre = c_out[s, 0:FAR, :].astype(F32) + dot(far_e[...], halo[0, N : 2 * N, :])
        for copy in mate_copies:
            copy.wait_recv()
        for q in range(1, nc):
            pre = pre + c_in[s, q].astype(F32)
        for k in (7, 8):
            for piece in range(4):
                arrived(i, halo, k, piece * CH, CH, piece)
        messages(halo, proc_w, CM, i, (7, 8), msg, pre)
        ahead, pushes = finish_step(i, own, proc_m, 7 * CM, 9 * CM + FAR)
        for copy in started + peer_copies + mate_copies + [to_partner]:
            copy.wait_send()

    for copy in weight_copies[3]:
        copy.wait()
    sent = dot(lat[...], ef[3, 0]).astype(BF)
    dec_out[...] = dot(dec_g[...], sent).astype(BF)
    dec_copies = []
    for b in others:
        span = pl.ds(b * CD, CD)
        copy = pltpu.make_async_remote_copy(
            dec_out.at[span], dec_in.at[span], d_ss.at[b], d_rs.at[b],
            device_id=target(b), device_id_type=MESH,
        )
        copy.start()
        dec_copies.append(copy)
    dec_in[4 * CD : 5 * CD, :] = dec_out[4 * CD : 5 * CD, :]
    own = grid_lat[...]
    receiver_part = dot(own, ef[3, 1]).astype(BF)
    near = dot(dec_e[...], receiver_part)
    start = dot(own, nf[3, 0])
    for copy in dec_copies:
        copy.wait_recv()
    pre = dec_in[...].astype(F32) + near
    y = dot(silu(pre), es[3])
    message = layer_norm(y, edge_gain[3:4, :]).astype(BF)
    out_copy.wait()
    final = node_update(3, own, dot(dec_m[...], message), start)
    out[...] = grid_in[...].astype(F32) + dot_nt(out_own[...], final)
    for copy in dec_copies:
        copy.wait_send()


def on_device(nr, nc, *args):
    vmem = pl.BlockSpec(memory_space=pltpu.VMEM)
    hbm = pl.BlockSpec(memory_space=pl.ANY)
    in_specs = [hbm] * 21
    args = list(args)
    args[4] = args[4].reshape(1, L)
    args[0] = args[0].T
    args[11] = args[11].T
    for at in (12, 15, 18):
        args[at] = jnp.transpose(args[at], (1, 0, 2))
    dma = pltpu.SemaphoreType.DMA
    nzx = nr // 2
    prediction = pl.pallas_call(
        functools.partial(body, nr, nc),
        out_shape=jax.ShapeDtypeStruct((CIN, G), F32),
        in_specs=in_specs,
        out_specs=vmem,
        scratch_shapes=[
            pltpu.VMEM((9, 1, CE), I32),
            pltpu.VMEM((9, 1, CM), I32),
            pltpu.VMEM((CIN, G), BF),
            pltpu.VMEM((CIN, L), BF),
            pltpu.VMEM((L, L), BF),
            pltpu.VMEM((1, L), F32),
            pltpu.VMEM((1, EM), I32),
            pltpu.VMEM((1, EM), I32),
            pltpu.VMEM((1, EE), I32),
            pltpu.VMEM((1, EE), I32),
            pltpu.VMEM((4, L), F32),
            pltpu.VMEM((4, L), F32),
            pltpu.VMEM((9, 1, CD), I32),
            pltpu.VMEM((1, ED), I32),
            pltpu.VMEM((1, ED), I32),
            pltpu.VMEM((4, 2, L, L), BF),
            pltpu.VMEM((4, L, L), BF),
            pltpu.VMEM((4, 2, L, L), BF),
            pltpu.VMEM((4, L, L), BF),
            pltpu.VMEM((N, L), BF),
            pltpu.VMEM((CIN, L), BF),
            pltpu.VMEM((9, 8, 128), I32),
            pltpu.VMEM((9, 8, 128), I32),
            pltpu.VMEM((2, 3, 8, 128), I32),
            pltpu.VMEM((128, 128), F32),
            pltpu.VMEM((2, 128, 128), I32),
            pltpu.VMEM((FAR, 128), I32),
            pltpu.VMEM((nc, FAR, 128), I32),
            pltpu.VMEM((nc * FAR, nr * CO), BF),
            pltpu.VMEM((1, EMP), I32),
            pltpu.VMEM((1, EMP), I32),
            pltpu.VMEM((16, 128), I32),
            pltpu.VMEM((9, G + N, L), BF),
            pltpu.VMEM((9, CE, G + N), BF),
            pltpu.VMEM((N, 9 * CE), BF),
            pltpu.VMEM((2, 9, 2 * N, L), BF),
            pltpu.VMEM((9, CM, 2 * N), BF),
            pltpu.VMEM((N, 9 * CM + FAR), BF),
            pltpu.VMEM((FAR, N), BF),
            pltpu.VMEM((2, nr * CO, L), BF),
            pltpu.VMEM((2, nc * FAR, L), BF),
            pltpu.VMEM((2, nc, FAR, L), BF),
            pltpu.VMEM((9 * CD, L), BF),
            pltpu.VMEM((640, L), BF),
            pltpu.VMEM((9 * CD, N), BF),
            pltpu.VMEM((640, G), BF),
            pltpu.VMEM((G, 640), BF),
            pltpu.VMEM((G, L), BF),
            pltpu.VMEM((N, L), BF),
            pltpu.VMEM((N, L), F32),
            pltpu.VMEM((N, L), F32),
            pltpu.VMEM((9 * CM + FAR, L), BF),
            dma((5, 4)),
            dma((15,)),
            dma((9,)),
            dma((9,)),
            dma((nc,)),
            dma((nc,)),
            dma((3, 9, 4)),
            dma((3, 9, 4)),
            dma((2, nzx)),
            dma((2, nzx)),
            dma((2,)),
            dma((2,)),
            dma((2, nc)),
            dma((2, nc)),
            dma((9,)),
            dma((9,)),
        ],
        compiler_params=pltpu.CompilerParams(
            collective_id=0, has_side_effects=True, vmem_limit_bytes=60 * 1024 * 1024
        ),
    )(*args)
    return prediction.T


def solution(mesh):
    both = ("row", "col")
    placed = (
        (P(both, None),) * 2
        + (P(),) * 10
        + (P(both, None, None), P(both, None), P(both, None)) * 3
    )
    return jax.shard_map(
        functools.partial(on_device, mesh.shape["row"], mesh.shape["col"]),
        mesh=mesh,
        in_specs=placed,
        out_specs=P(both, None),
        check_vma=False,
    )
```

```python
import functools

import jax
import jax.numpy as jnp
from jax import lax
from jax.experimental import pallas as pl
from jax.experimental.pallas import tpu as pltpu
from jax.sharding import PartitionSpec as P

BF = jnp.bfloat16
F32 = jnp.float32
I32 = jnp.int32
MESH = pl.DeviceIdType.MESH

L = 512
CIN = 227
G = 128
N = 320
CO = 16
FAR = 64
CE, CM, CD = 128, 256, 64
EE, EM, ED = 768, 1600, 384
EMP = 1664
FIRST_FAR = 9 * CM
EPSILON = 1e-05

PIECES = ((0, 64), (64, 64), (128, 128), (256, 64))
LAST = len(PIECES) - 1
CH = 80
GRID_PIECES = ((0, 64), (64, 64))


def dot(a, b):
    return jnp.dot(a, b, preferred_element_type=F32)


def dot_nt(a, b):
    return lax.dot_general(a, b, (((1,), (1,)), ((), ())), preferred_element_type=F32)


def iota(shape, dim):
    return lax.broadcasted_iota(I32, shape, dim)


def ones_where(cond):
    return jnp.where(cond, 1.0, 0.0).astype(BF)


def silu(v):
    u = 0.5 * v
    return (u + u * jnp.tanh(u)).astype(BF)


def layer_norm(y, gain):
    average = jnp.mean(y, axis=-1, keepdims=True)
    centered = y - average
    spread = jnp.mean(centered * centered, axis=-1, keepdims=True)
    return centered * lax.rsqrt(spread + EPSILON) * gain


def slot_receivers(slot, recv, high):
    edges = slot.shape[1]
    at_high = (slot >> 7) == iota((high, edges), 0)
    code = recv + 1
    first = jnp.where(at_high, (code >> 6).astype(F32), 0.0).astype(BF)
    second = jnp.where(at_high, (code & 63).astype(F32), 0.0).astype(BF)
    at_low = ones_where((slot & 127) == iota((128, edges), 0))
    rows = dot_nt(first, at_low) * 64.0 + dot_nt(second, at_low) - 1.0
    cols = dot_nt(at_low, first) * 64.0 + dot_nt(at_low, second) - 1.0
    return rows.astype(I32), cols.astype(I32)


def body(
    nr,
    nc,
    grid_in_any,
    mesh_init,
    embed_first_any,
    embed_second_any,
    embed_gain_any,
    edge_first_any,
    edge_second_any,
    edge_gain_any,
    node_first_any,
    node_second_any,
    node_gain_any,
    out_weight,
    enc_send_any,
    enc_slot_any,
    enc_recv_any,
    proc_send_any,
    proc_slot_any,
    proc_recv_any,
    dec_send_any,
    dec_slot_any,
    dec_recv_any,
    out,
    enc_send,
    proc_send,
    grid_in,
    embed_first,
    embed_second,
    embed_gain,
    proc_slot,
    proc_recv,
    enc_slot,
    enc_recv,
    edge_gain,
    node_gain,
    dec_send,
    dec_slot,
    dec_recv,
    ef,
    es,
    nf,
    ns,
    mesh_own,
    out_own,
    tab_out,
    tab_in,
    tab_side,
    tab_t,
    tab_cols,
    far_out,
    far_in,
    far_pick,
    slot_pad,
    recv_pad,
    slot_2d,
    enc_halo,
    enc_w,
    enc_m,
    proc_halo,
    proc_w,
    proc_m,
    far_e,
    gath,
    c_out,
    c_in,
    dec_out,
    dec_in,
    dec_g,
    dec_e,
    dec_m,
    grid_lat,
    lat,
    base,
    agg,
    msg,
    w_sem,
    in_sem,
    tab_ss,
    tab_rs,
    far_ss,
    far_rs,
    halo_ss,
    halo_rs,
    g_ss,
    g_rs,
    p_ss,
    p_rs,
    y_ss,
    y_rs,
    d_ss,
    d_rs,
):
    nzx = nr // 2
    r = lax.axis_index("row")
    c = lax.axis_index("col")
    core = lax.rem(r, 2)
    zx = r // 2
    up, down = lax.rem(r + 1, nr), lax.rem(r + nr - 1, nr)
    right, left = lax.rem(c + 1, nc), lax.rem(c + nc - 1, nc)
    rows_of = {-1: down, 0: r, 1: up}
    cols_of = {-1: left, 0: c, 1: right}
    partner = r + 1 - 2 * core

    def target(b):
        return (rows_of[b // 3 - 1], cols_of[b % 3 - 1])

    def peer(d):
        return (lax.rem(zx + d, nzx) * 2 + core, c)

    def mate(i):
        return (r, lax.rem(c + nc - i, nc))

    others = [b for b in range(9) if b != 4]
    first_core = core == 0
    x_row = r - 1 + 2 * core
    x_row = lax.rem(x_row + nr, nr)

    barrier = pltpu.get_barrier_semaphore()
    greeted = [(x_row, c)] + [peer(d) for d in range(1, nzx)]
    greeted += [mate(2), (r, left), (r, right), (partner, c)]
    for device in greeted:
        pl.semaphore_signal(barrier, inc=1, device_id=device, device_id_type=MESH)

    loads = []
    for at, (source, place) in enumerate(
        (
            (enc_send_any, enc_send),
            (proc_send_any, proc_send),
            (grid_in_any, grid_in),
            (embed_first_any, embed_first),
            (embed_second_any, embed_second),
            (embed_gain_any, embed_gain),
            (proc_slot_any, proc_slot),
            (proc_recv_any, proc_recv),
            (enc_slot_any, enc_slot),
            (enc_recv_any, enc_recv),
            (edge_gain_any, edge_gain),
            (node_gain_any, node_gain),
            (dec_send_any, dec_send),
            (dec_slot_any, dec_slot),
            (dec_recv_any, dec_recv),
        )
    ):
        copy = pltpu.make_async_copy(source, place, in_sem.at[at])
        copy.start()
        loads.append(copy)

    weight_copies = []
    for i in range(4):
        group = []
        for j, (source, place) in enumerate(
            (
                (edge_first_any, ef),
                (edge_second_any, es),
                (node_first_any, nf),
                (node_second_any, ns),
            )
        ):
            copy = pltpu.make_async_copy(source.at[i], place.at[i], w_sem.at[i, j])
            group.append(copy)
            if i == 0:
                copy.start()
        weight_copies.append(group)
        if i == 0:
            mesh_copies = [pltpu.make_async_copy(mesh_init, mesh_own, w_sem.at[4, 0])]
            mesh_copies[0].start()
    out_copy = pltpu.make_async_copy(out_weight, out_own, w_sem.at[4, 1])

    for copy in loads:
        copy.wait()

    toward_partner = 4 + 3 * (1 - 2 * core)
    toward_x = 4 - 3 * (1 - 2 * core)
    for at, b in enumerate(
        (4, toward_partner, toward_x)
        + (5, toward_partner + 1, toward_x + 1)
        + (3, toward_partner - 1, toward_x - 1)
    ):
        tab_out[at, 0:1, :] = enc_send[b]
        tab_out[at, 1:2, :] = proc_send[b, :, 0:128]
        tab_out[at, 2:3, :] = proc_send[b, :, 128:256]
        tab_out[at, 3:8, :] = jnp.zeros((5, 128), I32)

    hidden = silu(
        lax.dot_general(
            grid_in[...], embed_first[...], (((0,), (0,)), ((), ())), preferred_element_type=F32
        )
    )
    latent = layer_norm(dot(hidden, embed_second[...]), embed_gain[...]).astype(BF)
    grid_lat[...] = latent
    weight_copies[0][0].wait()
    enc_halo[0, 0:G, :] = dot(latent, ef[0, 0]).astype(BF)

    pl.semaphore_wait(barrier, len(greeted))

    tab_copies = []

    def send_tab(source, place, at, device):
        copy = pltpu.make_async_remote_copy(
            source, place, tab_ss.at[at], tab_rs.at[at], device_id=device, device_id_type=MESH
        )
        copy.start()
        tab_copies.append(copy)

    def send(step, halo, src, dst, first, count, piece, device, started):
        span = pl.ds(first, count)
        copy = pltpu.make_async_remote_copy(
            halo.at[src, span], halo.at[dst, span],
            halo_ss.at[step, dst, piece], halo_rs.at[step, dst, piece],
            device_id=device, device_id_type=MESH,
        )
        copy.start()
        started.append(copy)

    def arrived(step, halo, place, first, count, piece):
        rows = halo.at[place, pl.ds(first, count)]
        pltpu.make_async_copy(rows, rows, halo_rs.at[step, place, piece]).wait()

    def messages(halo, w, size, i, places, msg, extra=None):
        hidden = [silu(dot(w[k], halo[k])) for k in places]
        if extra is not None:
            hidden.append(silu(extra))
        y = dot(jnp.concatenate(hidden, axis=0), es[i])
        first = places[0] * size
        msg[first : first + y.shape[0], :] = layer_norm(y, edge_gain[i : i + 1, :]).astype(BF)

    def node_update(i, own, summed, start):
        node = start + dot(summed.astype(BF), nf[i, 1])
        update = layer_norm(dot(silu(node), ns[i]), node_gain[i : i + 1, :])
        return (own.astype(F32) + update).astype(BF)

    def begin_step(i, first, count, latents, started, pushes):
        s = i - 1
        halo = proc_halo.at[s]
        sent = dot(latents, ef[i, 0]).astype(BF)
        halo[0, first : first + count, :] = sent
        if first == 0:
            place = pl.ds(pl.multiple_of((core * nzx + zx) * CO, CO), CO)
            gath[s, place, :] = sent[0:CO, :]
            for d in range(1, nzx):
                copy = pltpu.make_async_remote_copy(
                    gath.at[s, place], gath.at[s, place],
                    g_ss.at[s, d], g_rs.at[s, d], device_id=peer(d), device_id_type=MESH,
                )
                copy.start()
                pushes.append(copy)
            pieces = (0,)
        else:
            send(i, halo, 0, 4, 3 * CH, CH, 3, (x_row, c), started)
            send(i, halo, 0, 4, 0, 3 * CH, 0, (x_row, c), started)
            send(i, halo, 0, 1, 0, N, 0, (partner, c), started)
            pieces = (1, 2, 3)
        for piece in pieces:
            send(i, halo, 0, 3, piece * CH, CH, piece, (r, right), started)
            send(i, halo, 0, 2, piece * CH, CH, piece, (r, left), started)

    def finish_step(i, own, m, first, last):
        started, pushes = [], []
        if i < 2:
            for copy in weight_copies[i + 1]:
                copy.wait()
        for at, count in ((0, CH), (CH, N - CH)):
            part = slice(at, at + count)
            summed = agg[part, :] + dot(m[part, first:last], msg[first:last, :])
            latents = node_update(i, own[part, :], summed, base[part, :])
            lat[part, :] = latents
            if i < 2:
                begin_step(i + 1, at, count, latents, started, pushes)
        return started, pushes

    def blocks_at(place):
        return ((4, 4), (1, 7), (3, 3), (5, 5), (7, 1), (0, 6), (2, 8), (6, 0), (8, 2))[place]

    def pick(place, take):
        one, two = blocks_at(place)
        return take(one) if one == two else jnp.where(first_core, take(one), take(two))

    started = []
    send_tab(tab_out.at[pl.ds(3, 3)], tab_side.at[1], 3, (r, right))
    send_tab(tab_out.at[pl.ds(6, 3)], tab_side.at[0], 2, (r, left))
    send_tab(tab_out.at[1], tab_in.at[1], 1, (partner, c))
    send_tab(tab_out.at[2], tab_in.at[4], 4, (x_row, c))
    for piece, (first, count) in enumerate(GRID_PIECES):
        send(0, enc_halo, 0, 3, first, count, piece, (r, right), started)
        send(0, enc_halo, 0, 2, first, count, piece, (r, left), started)
        if piece == 0:
            send(0, enc_halo, 0, 4, 0, G, 0, (x_row, c), started)
            send(0, enc_halo, 0, 1, 0, G, 0, (partner, c), started)

    for copy in mesh_copies:
        copy.wait()
    receiver_part = dot(mesh_own[...], ef[0, 1]).astype(BF)
    for k in range(9):
        enc_halo[k, G : G + N, :] = receiver_part

    slot_pad[...] = jnp.full((1, EMP), -1, I32)
    recv_pad[...] = jnp.zeros((1, EMP), I32)
    slot_pad[0:1, 0:EM] = proc_slot[...]
    recv_pad[0:1, 0:EM] = proc_recv[...]
    slot_2d[...] = jnp.full((16, 128), -1, I32)
    chunks = EMP // 128
    for i in range(chunks):
        slot_2d[i : i + 1, :] = slot_pad[0:1, i * 128 : (i + 1) * 128]
    is_far = slot_2d[...] >= FIRST_FAR
    far_ones = ones_where(is_far)
    within = dot(far_ones, ones_where(iota((128, 128), 0) <= iota((128, 128), 1)))
    above = dot(ones_where(iota((16, 16), 1) < iota((16, 16), 0)), far_ones)
    rank = within + jnp.sum(above, axis=1, keepdims=True) - 1.0
    rank = jnp.where(is_far, rank.astype(I32), -1)
    picks = jnp.concatenate(
        [ones_where(rank[i : i + 1, :] == iota((FAR, 128), 0)) for i in range(chunks)], axis=1
    )
    node = jnp.maximum(slot_pad[...] - FIRST_FAR, 0)
    row_id = iota((8, EMP), 0)
    values = jnp.where(
        row_id == 0,
        node >> 6,
        jnp.where(
            row_id == 1,
            node & 63,
            jnp.where(row_id == 2, recv_pad[...] >> 6, jnp.where(row_id == 3, recv_pad[...] & 63, 0)),
        ),
    )
    values = values.astype(F32).astype(BF)
    far_cols = dot_nt(picks, values)
    far_rows = dot_nt(values, picks)
    far_node = (far_cols[:, 0:1] * 64.0 + far_cols[:, 1:2]).astype(I32)
    far_out[...] = jnp.broadcast_to(far_node, (FAR, 128))
    far_in[0] = jnp.broadcast_to(far_node, (FAR, 128))
    far_copies = []
    for i in range(1, nc):
        copy = pltpu.make_async_remote_copy(
            far_out, far_in.at[nc - i], far_ss.at[nc - i], far_rs.at[nc - i],
            device_id=mate(i), device_id_type=MESH,
        )
        copy.start()
        far_copies.append(copy)
    far_recv_col = (far_cols[:, 2:3] * 64.0 + far_cols[:, 3:4]).astype(I32)
    far_recv_row = (far_rows[2:3, :] * 64.0 + far_rows[3:4, :]).astype(I32)
    far_e[...] = ones_where(far_recv_col == iota((FAR, N), 1))
    proc_m[:, 9 * CM :] = ones_where(far_recv_row == iota((N, FAR), 0))

    enc_rows, enc_cols = slot_receivers(enc_slot[...], enc_recv[...], 16)
    for k in range(9):
        receiver = pick(k, lambda b: enc_rows[b : b + 1, :])
        enc_m[:, k * CE : (k + 1) * CE] = ones_where(receiver == iota((N, CE), 0))

    def tables(places, at):
        first, count = places[0], len(places)
        tab_t[0 : 8 * count, :] = tab_in[first : first + count].reshape(8 * count, 128).astype(F32)
        tab_t[8 * count :, :] = jnp.zeros((128 - 8 * count, 128), F32)
        tab_cols[at] = jnp.transpose(tab_t[...]).astype(I32)

    def enc_matrices(places, at):
        for k in places:
            here = iota((CE, G + N), 1)
            receiver = pick(k, lambda b: enc_cols[:, b : b + 1])
            receiver = jnp.where(receiver < 0, -1, receiver + G)
            column = 8 * (k - places[0])
            sender = tab_cols[at, :, column : column + 1]
            enc_w[k] = ones_where((here == sender) | (here == receiver))

    def proc_matrices(places, at):
        for k in places:
            here = iota((128, 2 * N), 1)
            for half in range(2):
                receiver = pick(k, lambda b: proc_cols[:, 2 * b + half : 2 * b + half + 1])
                receiver = jnp.where(receiver < 0, -1, receiver + N)
                column = 8 * (k - places[0]) + 1 + half
                sender = tab_cols[at, :, column : column + 1]
                span = slice(half * 128, (half + 1) * 128)
                proc_w[k, span, :] = ones_where((here == sender) | (here == receiver))

    def dec_matrices():
        dec_rows, dec_cols = slot_receivers(dec_slot[...], dec_recv[...], 16)
        for h in range(5):
            span = slice(h * 128, (h + 1) * 128)
            dec_e[span, :] = ones_where(dec_cols[:, h : h + 1] == iota((128, G), 1))
            dec_m[:, span] = ones_where(dec_rows[h : h + 1, :] == iota((G, 128), 0))
        tab_t[...] = jnp.zeros((128, 128), F32)
        for b in range(9):
            tab_t[b : b + 1, 0:CD] = dec_send[b].astype(F32)
        dec_tabs = jnp.transpose(tab_t[...]).astype(I32)
        for b in range(9):
            dec_g[b * CD : (b + 1) * CD, :] = ones_where(dec_tabs[0:CD, b : b + 1] == iota((CD, N), 1))
        dec_in[9 * CD : 640, :] = jnp.zeros((64, L), BF)

    for group in weight_copies[1:]:
        for copy in group:
            copy.start()
    out_copy.start()
    tab_copies[0].wait_recv()
    tab_copies[1].wait_recv()
    send_tab(tab_side.at[0, 1], tab_in.at[5], 5, (partner, c))
    send_tab(tab_side.at[0, 2], tab_in.at[7], 7, (x_row, c))
    send_tab(tab_side.at[1, 1], tab_in.at[6], 6, (partner, c))
    send_tab(tab_side.at[1, 2], tab_in.at[8], 8, (x_row, c))
    tab_in[0] = tab_out[0]
    tab_in[2] = tab_side[0, 0]
    tab_in[3] = tab_side[1, 0]
    for piece, (first, count) in enumerate(GRID_PIECES):
        arrived(0, enc_halo, 2, first, count, piece)
        send(0, enc_halo, 2, 7, first, count, piece, (x_row, c), started)
        arrived(0, enc_halo, 3, first, count, piece)
        send(0, enc_halo, 3, 8, first, count, piece, (x_row, c), started)
    send(0, enc_halo, 2, 5, 0, G, 0, (partner, c), started)
    send(0, enc_halo, 3, 6, 0, G, 0, (partner, c), started)
    tab_copies[2].wait_recv()
    tab_copies[3].wait_recv()
    near = (0, 1, 2, 3, 4)
    tables(near, 0)
    enc_matrices(near, 0)
    for copy in weight_copies[0][1:]:
        copy.wait()
    arrived(0, enc_halo, 1, 0, G, 0)
    arrived(0, enc_halo, 4, 0, G, 0)
    messages(enc_halo, enc_w, CE, 0, near, msg)
    base[...] = dot(mesh_own[...], nf[0, 0])
    for copy in tab_copies[4:]:
        copy.wait_recv()
    diagonal = (5, 6, 7, 8)
    tables(diagonal, 1)
    enc_matrices(diagonal, 1)
    arrived(0, enc_halo, 5, 0, G, 0)
    arrived(0, enc_halo, 6, 0, G, 0)
    messages(enc_halo, enc_w, CE, 0, (5, 6), msg)
    agg[...] = dot(enc_m[:, 0 : 7 * CE], msg[0 : 7 * CE, :])

    proc_rows, proc_cols = slot_receivers(slot_pad[...], recv_pad[...], 24)
    for k in range(9):
        for half in range(2):
            receiver = pick(k, lambda b: proc_rows[2 * b + half : 2 * b + half + 1, :])
            first = k * CM + half * 128
            proc_m[:, first : first + 128] = ones_where(receiver == iota((N, 128), 0))
    proc_matrices(near, 0)
    dec_matrices()
    for copy in far_copies:
        copy.wait_recv()
    found = []
    for q in range(nc):
        number = far_in[q]
        device = number // CO
        band = device // nc
        index = (band % 2) * (nzx * CO) + (band // 2) * CO + number % CO
        index = jnp.where(device % nc == c, index, -1)
        found.append(
            jnp.concatenate(
                [ones_where(index == iota((FAR, 128), 1) + 128 * t) for t in range(max(1, nr * CO // 128))],
                axis=1,
            )
        )
    far_pick[...] = jnp.concatenate(found, axis=0)

    for k in (7, 8):
        for piece, (first, count) in enumerate(GRID_PIECES):
            arrived(0, enc_halo, k, first, count, piece)
    messages(enc_halo, enc_w, CE, 0, (7, 8), msg)
    ahead, pushes = finish_step(0, mesh_own[...], enc_m, 7 * CE, 9 * CE)
    for copy in started + tab_copies + far_copies:
        copy.wait_send()

    for s in range(2):
        i = s + 1
        halo = proc_halo.at[s]
        own = lat[...]
        started, peer_copies = ahead, pushes
        receiver_part = dot(own, ef[i, 1]).astype(BF)
        for k in range(9):
            halo[k, N : 2 * N, :] = receiver_part
        base[...] = dot(own, nf[i, 0])
        arrived(i, halo, 1, 0, N, 0)
        messages(halo, proc_w, CM, i, (0, 1), msg)
        for piece in range(3):
            arrived(i, halo, 2, piece * CH, CH, piece)
            send(i, halo, 2, 7, piece * CH, CH, piece, (x_row, c), started)
            arrived(i, halo, 3, piece * CH, CH, piece)
            send(i, halo, 3, 8, piece * CH, CH, piece, (x_row, c), started)
            if piece == 1:
                arrived(i, halo, 4, 3 * CH, CH, 3)
                send(i, halo, 4, 8, 3 * CH, CH, 3, (r, right), started)
                send(i, halo, 4, 7, 3 * CH, CH, 3, (r, left), started)
                for copy in peer_copies:
                    copy.wait_recv()
                mine = pl.ds(pl.multiple_of(core * (nzx * CO), CO), nzx * CO)
                to_partner = pltpu.make_async_remote_copy(
                    gath.at[s, mine], gath.at[s, mine], p_ss.at[s], p_rs.at[s],
                    device_id=(partner, c), device_id_type=MESH,
                )
                to_partner.start()
        to_partner.wait_recv()
        chosen = dot(far_pick[...], gath[s]).astype(BF)
        c_out[s] = chosen
        mate_copies = []
        for q in range(1, nc):
            copy = pltpu.make_async_remote_copy(
                c_out.at[s, pl.ds(q * FAR, FAR)], c_in.at[s, q], y_ss.at[s, q], y_rs.at[s, q],
                device_id=mate(q), device_id_type=MESH,
            )
            copy.start()
            mate_copies.append(copy)

        arrived(i, halo, 2, 3 * CH, CH, 3)
        send(i, halo, 2, 5, 0, N, 0, (partner, c), started)
        arrived(i, halo, 3, 3 * CH, CH, 3)
        send(i, halo, 3, 6, 0, N, 0, (partner, c), started)
        messages(halo, proc_w, CM, i, (2, 3), msg)
        if s == 0:
            proc_matrices(diagonal, 1)
        arrived(i, halo, 4, 0, 3 * CH, 0)
        for k in (5, 6):
            arrived(i, halo, k, 0, N, 0)
        messages(halo, proc_w, CM, i, (4, 5, 6), msg)
        agg[...] = dot(proc_m[:, 0 : 7 * CM], msg[0 : 7 * CM, :])
        pre = c_out[s, 0:FAR, :].astype(F32) + dot(far_e[...], halo[0, N : 2 * N, :])
        for copy in mate_copies:
            copy.wait_recv()
        for q in range(1, nc):
            pre = pre + c_in[s, q].astype(F32)
        for k in (7, 8):
            for piece in range(4):
                arrived(i, halo, k, piece * CH, CH, piece)
        messages(halo, proc_w, CM, i, (7, 8), msg, pre)
        ahead, pushes = finish_step(i, own, proc_m, 7 * CM, 9 * CM + FAR)
        for copy in started + peer_copies + mate_copies + [to_partner]:
            copy.wait_send()

    for copy in weight_copies[3]:
        copy.wait()
    sent = dot(lat[...], ef[3, 0]).astype(BF)
    dec_out[...] = dot(dec_g[...], sent).astype(BF)
    dec_copies = []
    for b in others:
        span = pl.ds(b * CD, CD)
        copy = pltpu.make_async_remote_copy(
            dec_out.at[span], dec_in.at[span], d_ss.at[b], d_rs.at[b],
            device_id=target(b), device_id_type=MESH,
        )
        copy.start()
        dec_copies.append(copy)
    dec_in[4 * CD : 5 * CD, :] = dec_out[4 * CD : 5 * CD, :]
    own = grid_lat[...]
    receiver_part = dot(own, ef[3, 1]).astype(BF)
    near = dot(dec_e[...], receiver_part)
    start = dot(own, nf[3, 0])
    for copy in dec_copies:
        copy.wait_recv()
    pre = dec_in[...].astype(F32) + near
    y = dot(silu(pre), es[3])
    message = layer_norm(y, edge_gain[3:4, :]).astype(BF)
    out_copy.wait()
    final = node_update(3, own, dot(dec_m[...], message), start)
    out[...] = grid_in[...].astype(F32) + dot_nt(out_own[...], final)
    for copy in dec_copies:
        copy.wait_send()


def on_device(nr, nc, *args):
    vmem = pl.BlockSpec(memory_space=pltpu.VMEM)
    hbm = pl.BlockSpec(memory_space=pl.ANY)
    in_specs = [hbm] * 21
    args = list(args)
    args[4] = args[4].reshape(1, L)
    args[0] = args[0].T
    args[11] = args[11].T
    for at in (12, 15, 18):
        args[at] = jnp.transpose(args[at], (1, 0, 2))
    dma = pltpu.SemaphoreType.DMA
    nzx = nr // 2
    prediction = pl.pallas_call(
        functools.partial(body, nr, nc),
        out_shape=jax.ShapeDtypeStruct((CIN, G), F32),
        in_specs=in_specs,
        out_specs=vmem,
        scratch_shapes=[
            pltpu.VMEM((9, 1, CE), I32),
            pltpu.VMEM((9, 1, CM), I32),
            pltpu.VMEM((CIN, G), BF),
            pltpu.VMEM((CIN, L), BF),
            pltpu.VMEM((L, L), BF),
            pltpu.VMEM((1, L), F32),
            pltpu.VMEM((1, EM), I32),
            pltpu.VMEM((1, EM), I32),
            pltpu.VMEM((1, EE), I32),
            pltpu.VMEM((1, EE), I32),
            pltpu.VMEM((4, L), F32),
            pltpu.VMEM((4, L), F32),
            pltpu.VMEM((9, 1, CD), I32),
            pltpu.VMEM((1, ED), I32),
            pltpu.VMEM((1, ED), I32),
            pltpu.VMEM((4, 2, L, L), BF),
            pltpu.VMEM((4, L, L), BF),
            pltpu.VMEM((4, 2, L, L), BF),
            pltpu.VMEM((4, L, L), BF),
            pltpu.VMEM((N, L), BF),
            pltpu.VMEM((CIN, L), BF),
            pltpu.VMEM((9, 8, 128), I32),
            pltpu.VMEM((9, 8, 128), I32),
            pltpu.VMEM((2, 3, 8, 128), I32),
            pltpu.VMEM((128, 128), F32),
            pltpu.VMEM((2, 128, 128), I32),
            pltpu.VMEM((FAR, 128), I32),
            pltpu.VMEM((nc, FAR, 128), I32),
            pltpu.VMEM((nc * FAR, nr * CO), BF),
            pltpu.VMEM((1, EMP), I32),
            pltpu.VMEM((1, EMP), I32),
            pltpu.VMEM((16, 128), I32),
            pltpu.VMEM((9, G + N, L), BF),
            pltpu.VMEM((9, CE, G + N), BF),
            pltpu.VMEM((N, 9 * CE), BF),
            pltpu.VMEM((2, 9, 2 * N, L), BF),
            pltpu.VMEM((9, CM, 2 * N), BF),
            pltpu.VMEM((N, 9 * CM + FAR), BF),
            pltpu.VMEM((FAR, N), BF),
            pltpu.VMEM((2, nr * CO, L), BF),
            pltpu.VMEM((2, nc * FAR, L), BF),
            pltpu.VMEM((2, nc, FAR, L), BF),
            pltpu.VMEM((9 * CD, L), BF),
            pltpu.VMEM((640, L), BF),
            pltpu.VMEM((9 * CD, N), BF),
            pltpu.VMEM((640, G), BF),
            pltpu.VMEM((G, 640), BF),
            pltpu.VMEM((G, L), BF),
            pltpu.VMEM((N, L), BF),
            pltpu.VMEM((N, L), F32),
            pltpu.VMEM((N, L), F32),
            pltpu.VMEM((9 * CM + FAR, L), BF),
            dma((5, 4)),
            dma((15,)),
            dma((9,)),
            dma((9,)),
            dma((nc,)),
            dma((nc,)),
            dma((3, 9, 4)),
            dma((3, 9, 4)),
            dma((2, nzx)),
            dma((2, nzx)),
            dma((2,)),
            dma((2,)),
            dma((2, nc)),
            dma((2, nc)),
            dma((9,)),
            dma((9,)),
        ],
        compiler_params=pltpu.CompilerParams(
            collective_id=0, has_side_effects=True, vmem_limit_bytes=60 * 1024 * 1024
        ),
    )(*args)
    return prediction.T


def solution(mesh):
    both = ("row", "col")
    placed = (
        (P(both, None),) * 2
        + (P(),) * 10
        + (P(both, None, None), P(both, None), P(both, None)) * 3
    )
    return jax.shard_map(
        functools.partial(on_device, mesh.shape["row"], mesh.shape["col"]),
        mesh=mesh,
        in_specs=placed,
        out_specs=P(both, None),
        check_vma=False,
    )
```

```python
import functools

import jax
import jax.numpy as jnp
from jax import lax
from jax.experimental import pallas as pl
from jax.experimental.pallas import tpu as pltpu
from jax.sharding import PartitionSpec as P

BF = jnp.bfloat16
F32 = jnp.float32
I32 = jnp.int32
MESH = pl.DeviceIdType.MESH

L = 512
CIN = 227
G = 128
N = 320
CO = 16
FAR = 64
CE, CM, CD = 128, 256, 64
EE, EM, ED = 768, 1600, 384
EMP = 1664
FIRST_FAR = 9 * CM
EPSILON = 1e-05

PIECES = ((0, 64), (64, 64), (128, 128), (256, 64))
LAST = len(PIECES) - 1
CH = 80
GRID_PIECES = ((0, 64), (64, 64))


def dot(a, b):
    return jnp.dot(a, b, preferred_element_type=F32)


def dot_nt(a, b):
    return lax.dot_general(a, b, (((1,), (1,)), ((), ())), preferred_element_type=F32)


def iota(shape, dim):
    return lax.broadcasted_iota(I32, shape, dim)


def ones_where(cond):
    return jnp.where(cond, 1.0, 0.0).astype(BF)


def silu(v):
    u = 0.5 * v
    return (u + u * jnp.tanh(u)).astype(BF)


def layer_norm(y, gain):
    average = jnp.mean(y, axis=-1, keepdims=True)
    centered = y - average
    spread = jnp.mean(centered * centered, axis=-1, keepdims=True)
    return centered * lax.rsqrt(spread + EPSILON) * gain


def slot_receivers(slot, recv, high):
    edges = slot.shape[1]
    at_high = (slot >> 7) == iota((high, edges), 0)
    code = recv + 1
    first = jnp.where(at_high, (code >> 6).astype(F32), 0.0).astype(BF)
    second = jnp.where(at_high, (code & 63).astype(F32), 0.0).astype(BF)
    at_low = ones_where((slot & 127) == iota((128, edges), 0))
    rows = dot_nt(first, at_low) * 64.0 + dot_nt(second, at_low) - 1.0
    cols = dot_nt(at_low, first) * 64.0 + dot_nt(at_low, second) - 1.0
    return rows.astype(I32), cols.astype(I32)


def body(
    nr,
    nc,
    grid_in_any,
    mesh_init,
    embed_first_any,
    embed_second_any,
    embed_gain_any,
    edge_first_any,
    edge_second_any,
    edge_gain_any,
    node_first_any,
    node_second_any,
    node_gain_any,
    out_weight,
    enc_send_any,
    enc_slot_any,
    enc_recv_any,
    proc_send_any,
    proc_slot_any,
    proc_recv_any,
    dec_send_any,
    dec_slot_any,
    dec_recv_any,
    out,
    enc_send,
    proc_send,
    grid_in,
    embed_first,
    embed_second,
    embed_gain,
    proc_slot,
    proc_recv,
    enc_slot,
    enc_recv,
    edge_gain,
    node_gain,
    dec_send,
    dec_slot,
    dec_recv,
    ef,
    es,
    nf,
    ns,
    mesh_own,
    out_own,
    tab_out,
    tab_in,
    tab_side,
    tab_t,
    tab_cols,
    far_out,
    far_in,
    far_pick,
    slot_pad,
    recv_pad,
    slot_2d,
    enc_halo,
    enc_w,
    enc_m,
    proc_halo,
    proc_w,
    proc_m,
    far_e,
    gath,
    c_out,
    c_in,
    dec_out,
    dec_in,
    dec_g,
    dec_e,
    dec_m,
    grid_lat,
    lat,
    base,
    agg,
    msg,
    w_sem,
    in_sem,
    tab_ss,
    tab_rs,
    far_ss,
    far_rs,
    halo_ss,
    halo_rs,
    g_ss,
    g_rs,
    p_ss,
    p_rs,
    y_ss,
    y_rs,
    d_ss,
    d_rs,
):
    nzx = nr // 2
    r = lax.axis_index("row")
    c = lax.axis_index("col")
    core = lax.rem(r, 2)
    zx = r // 2
    up, down = lax.rem(r + 1, nr), lax.rem(r + nr - 1, nr)
    right, left = lax.rem(c + 1, nc), lax.rem(c + nc - 1, nc)
    rows_of = {-1: down, 0: r, 1: up}
    cols_of = {-1: left, 0: c, 1: right}
    partner = r + 1 - 2 * core

    def target(b):
        return (rows_of[b // 3 - 1], cols_of[b % 3 - 1])

    def peer(d):
        return (lax.rem(zx + d, nzx) * 2 + core, c)

    def mate(i):
        return (r, lax.rem(c + nc - i, nc))

    others = [b for b in range(9) if b != 4]
    first_core = core == 0
    x_row = r - 1 + 2 * core
    x_row = lax.rem(x_row + nr, nr)

    barrier = pltpu.get_barrier_semaphore()
    greeted = [(x_row, c)] + [peer(d) for d in range(1, nzx)]
    greeted += [mate(2), (r, left), (r, right), (partner, c)]
    for device in greeted:
        pl.semaphore_signal(barrier, inc=1, device_id=device, device_id_type=MESH)

    loads = []
    for at, (source, place) in enumerate(
        (
            (enc_send_any, enc_send),
            (proc_send_any, proc_send),
            (grid_in_any, grid_in),
            (embed_first_any, embed_first),
            (embed_second_any, embed_second),
            (embed_gain_any, embed_gain),
            (proc_slot_any, proc_slot),
            (proc_recv_any, proc_recv),
            (enc_slot_any, enc_slot),
            (enc_recv_any, enc_recv),
            (edge_gain_any, edge_gain),
            (node_gain_any, node_gain),
            (dec_send_any, dec_send),
            (dec_slot_any, dec_slot),
            (dec_recv_any, dec_recv),
        )
    ):
        copy = pltpu.make_async_copy(source, place, in_sem.at[at])
        copy.start()
        loads.append(copy)

    weight_copies = []
    for i in range(4):
        group = []
        for j, (source, place) in enumerate(
            (
                (edge_first_any, ef),
                (edge_second_any, es),
                (node_first_any, nf),
                (node_second_any, ns),
            )
        ):
            copy = pltpu.make_async_copy(source.at[i], place.at[i], w_sem.at[i, j])
            group.append(copy)
            if i == 0:
                copy.start()
        weight_copies.append(group)
        if i == 0:
            mesh_copies = [pltpu.make_async_copy(mesh_init, mesh_own, w_sem.at[4, 0])]
            mesh_copies[0].start()
    out_copy = pltpu.make_async_copy(out_weight, out_own, w_sem.at[4, 1])

    for copy in loads:
        copy.wait()

    toward_partner = 4 + 3 * (1 - 2 * core)
    toward_x = 4 - 3 * (1 - 2 * core)
    for at, b in enumerate(
        (4, toward_partner, toward_x)
        + (5, toward_partner + 1, toward_x + 1)
        + (3, toward_partner - 1, toward_x - 1)
    ):
        tab_out[at, 0:1, :] = enc_send[b]
        tab_out[at, 1:2, :] = proc_send[b, :, 0:128]
        tab_out[at, 2:3, :] = proc_send[b, :, 128:256]
        tab_out[at, 3:8, :] = jnp.zeros((5, 128), I32)

    hidden = silu(
        lax.dot_general(
            grid_in[...], embed_first[...], (((0,), (0,)), ((), ())), preferred_element_type=F32
        )
    )
    latent = layer_norm(dot(hidden, embed_second[...]), embed_gain[...]).astype(BF)
    grid_lat[...] = latent
    weight_copies[0][0].wait()
    enc_halo[0, 0:G, :] = dot(latent, ef[0, 0]).astype(BF)

    pl.semaphore_wait(barrier, len(greeted))

    tab_copies = []

    def send_tab(source, place, at, device):
        copy = pltpu.make_async_remote_copy(
            source, place, tab_ss.at[at], tab_rs.at[at], device_id=device, device_id_type=MESH
        )
        copy.start()
        tab_copies.append(copy)

    def send(step, halo, src, dst, first, count, piece, device, started):
        span = pl.ds(first, count)
        copy = pltpu.make_async_remote_copy(
            halo.at[src, span], halo.at[dst, span],
            halo_ss.at[step, dst, piece], halo_rs.at[step, dst, piece],
            device_id=device, device_id_type=MESH,
        )
        copy.start()
        started.append(copy)

    def arrived(step, halo, place, first, count, piece):
        rows = halo.at[place, pl.ds(first, count)]
        pltpu.make_async_copy(rows, rows, halo_rs.at[step, place, piece]).wait()

    def messages(halo, w, size, i, places, msg, extra=None):
        hidden = [silu(dot(w[k], halo[k])) for k in places]
        if extra is not None:
            hidden.append(silu(extra))
        y = dot(jnp.concatenate(hidden, axis=0), es[i])
        first = places[0] * size
        msg[first : first + y.shape[0], :] = layer_norm(y, edge_gain[i : i + 1, :]).astype(BF)

    def node_update(i, own, summed, start):
        node = start + dot(summed.astype(BF), nf[i, 1])
        update = layer_norm(dot(silu(node), ns[i]), node_gain[i : i + 1, :])
        return (own.astype(F32) + update).astype(BF)

    def begin_step(i, first, count, latents, started, pushes):
        s = i - 1
        halo = proc_halo.at[s]
        sent = dot(latents, ef[i, 0]).astype(BF)
        halo[0, first : first + count, :] = sent
        if first == 0:
            place = pl.ds(pl.multiple_of((core * nzx + zx) * CO, CO), CO)
            gath[s, place, :] = sent[0:CO, :]
            for d in range(1, nzx):
                copy = pltpu.make_async_remote_copy(
                    gath.at[s, place], gath.at[s, place],
                    g_ss.at[s, d], g_rs.at[s, d], device_id=peer(d), device_id_type=MESH,
                )
                copy.start()
                pushes.append(copy)
            pieces = (0,)
        else:
            send(i, halo, 0, 4, 3 * CH, CH, 3, (x_row, c), started)
            send(i, halo, 0, 4, 0, 3 * CH, 0, (x_row, c), started)
            send(i, halo, 0, 1, 0, N, 0, (partner, c), started)
            pieces = (1, 2, 3)
        for piece in pieces:
            send(i, halo, 0, 3, piece * CH, CH, piece, (r, right), started)
            send(i, halo, 0, 2, piece * CH, CH, piece, (r, left), started)

    def finish_step(i, own, m, first, last):
        started, pushes = [], []
        if i < 2:
            for copy in weight_copies[i + 1]:
                copy.wait()
        for at, count in ((0, CH), (CH, N - CH)):
            part = slice(at, at + count)
            summed = agg[part, :] + dot(m[part, first:last], msg[first:last, :])
            latents = node_update(i, own[part, :], summed, base[part, :])
            lat[part, :] = latents
            if i < 2:
                begin_step(i + 1, at, count, latents, started, pushes)
        return started, pushes

    def blocks_at(place):
        return ((4, 4), (1, 7), (3, 3), (5, 5), (7, 1), (0, 6), (2, 8), (6, 0), (8, 2))[place]

    def pick(place, take):
        one, two = blocks_at(place)
        return take(one) if one == two else jnp.where(first_core, take(one), take(two))

    started = []
    send_tab(tab_out.at[pl.ds(3, 3)], tab_side.at[1], 3, (r, right))
    send_tab(tab_out.at[pl.ds(6, 3)], tab_side.at[0], 2, (r, left))
    send_tab(tab_out.at[1], tab_in.at[1], 1, (partner, c))
    send_tab(tab_out.at[2], tab_in.at[4], 4, (x_row, c))
    for piece, (first, count) in enumerate(GRID_PIECES):
        send(0, enc_halo, 0, 3, first, count, piece, (r, right), started)
        send(0, enc_halo, 0, 2, first, count, piece, (r, left), started)
        if piece == 0:
            send(0, enc_halo, 0, 4, 0, G, 0, (x_row, c), started)
            send(0, enc_halo, 0, 1, 0, G, 0, (partner, c), started)

    for copy in mesh_copies:
        copy.wait()
    receiver_part = dot(mesh_own[...], ef[0, 1]).astype(BF)
    for k in range(9):
        enc_halo[k, G : G + N, :] = receiver_part

    slot_pad[...] = jnp.full((1, EMP), -1, I32)
    recv_pad[...] = jnp.zeros((1, EMP), I32)
    slot_pad[0:1, 0:EM] = proc_slot[...]
    recv_pad[0:1, 0:EM] = proc_recv[...]
    slot_2d[...] = jnp.full((16, 128), -1, I32)
    chunks = EMP // 128
    for i in range(chunks):
        slot_2d[i : i + 1, :] = slot_pad[0:1, i * 128 : (i + 1) * 128]
    is_far = slot_2d[...] >= FIRST_FAR
    far_ones = ones_where(is_far)
    within = dot(far_ones, ones_where(iota((128, 128), 0) <= iota((128, 128), 1)))
    above = dot(ones_where(iota((16, 16), 1) < iota((16, 16), 0)), far_ones)
    rank = within + jnp.sum(above, axis=1, keepdims=True) - 1.0
    rank = jnp.where(is_far, rank.astype(I32), -1)
    picks = jnp.concatenate(
        [ones_where(rank[i : i + 1, :] == iota((FAR, 128), 0)) for i in range(chunks)], axis=1
    )
    node = jnp.maximum(slot_pad[...] - FIRST_FAR, 0)
    row_id = iota((8, EMP), 0)
    values = jnp.where(
        row_id == 0,
        node >> 6,
        jnp.where(
            row_id == 1,
            node & 63,
            jnp.where(row_id == 2, recv_pad[...] >> 6, jnp.where(row_id == 3, recv_pad[...] & 63, 0)),
        ),
    )
    values = values.astype(F32).astype(BF)
    far_cols = dot_nt(picks, values)
    far_rows = dot_nt(values, picks)
    far_node = (far_cols[:, 0:1] * 64.0 + far_cols[:, 1:2]).astype(I32)
    far_out[...] = jnp.broadcast_to(far_node, (FAR, 128))
    far_in[0] = jnp.broadcast_to(far_node, (FAR, 128))
    far_copies = []
    for i in range(1, nc):
        copy = pltpu.make_async_remote_copy(
            far_out, far_in.at[nc - i], far_ss.at[nc - i], far_rs.at[nc - i],
            device_id=mate(i), device_id_type=MESH,
        )
        copy.start()
        far_copies.append(copy)
    far_recv_col = (far_cols[:, 2:3] * 64.0 + far_cols[:, 3:4]).astype(I32)
    far_recv_row = (far_rows[2:3, :] * 64.0 + far_rows[3:4, :]).astype(I32)
    far_e[...] = ones_where(far_recv_col == iota((FAR, N), 1))
    proc_m[:, 9 * CM :] = ones_where(far_recv_row == iota((N, FAR), 0))

    enc_rows, enc_cols = slot_receivers(enc_slot[...], enc_recv[...], 16)
    for k in range(9):
        receiver = pick(k, lambda b: enc_rows[b : b + 1, :])
        enc_m[:, k * CE : (k + 1) * CE] = ones_where(receiver == iota((N, CE), 0))

    def tables(places, at):
        first, count = places[0], len(places)
        tab_t[0 : 8 * count, :] = tab_in[first : first + count].reshape(8 * count, 128).astype(F32)
        tab_t[8 * count :, :] = jnp.zeros((128 - 8 * count, 128), F32)
        tab_cols[at] = jnp.transpose(tab_t[...]).astype(I32)

    def enc_matrices(places, at):
        for k in places:
            here = iota((CE, G + N), 1)
            receiver = pick(k, lambda b: enc_cols[:, b : b + 1])
            receiver = jnp.where(receiver < 0, -1, receiver + G)
            column = 8 * (k - places[0])
            sender = tab_cols[at, :, column : column + 1]
            enc_w[k] = ones_where((here == sender) | (here == receiver))

    def proc_matrices(places, at):
        for k in places:
            here = iota((128, 2 * N), 1)
            for half in range(2):
                receiver = pick(k, lambda b: proc_cols[:, 2 * b + half : 2 * b + half + 1])
                receiver = jnp.where(receiver < 0, -1, receiver + N)
                column = 8 * (k - places[0]) + 1 + half
                sender = tab_cols[at, :, column : column + 1]
                span = slice(half * 128, (half + 1) * 128)
                proc_w[k, span, :] = ones_where((here == sender) | (here == receiver))

    def dec_matrices():
        dec_rows, dec_cols = slot_receivers(dec_slot[...], dec_recv[...], 16)
        for h in range(5):
            span = slice(h * 128, (h + 1) * 128)
            dec_e[span, :] = ones_where(dec_cols[:, h : h + 1] == iota((128, G), 1))
            dec_m[:, span] = ones_where(dec_rows[h : h + 1, :] == iota((G, 128), 0))
        tab_t[...] = jnp.zeros((128, 128), F32)
        for b in range(9):
            tab_t[b : b + 1, 0:CD] = dec_send[b].astype(F32)
        dec_tabs = jnp.transpose(tab_t[...]).astype(I32)
        for b in range(9):
            dec_g[b * CD : (b + 1) * CD, :] = ones_where(dec_tabs[0:CD, b : b + 1] == iota((CD, N), 1))
        dec_in[9 * CD : 640, :] = jnp.zeros((64, L), BF)

    for group in weight_copies[1:]:
        for copy in group:
            copy.start()
    out_copy.start()
    tab_copies[0].wait_recv()
    tab_copies[1].wait_recv()
    send_tab(tab_side.at[0, 1], tab_in.at[5], 5, (partner, c))
    send_tab(tab_side.at[0, 2], tab_in.at[7], 7, (x_row, c))
    send_tab(tab_side.at[1, 1], tab_in.at[6], 6, (partner, c))
    send_tab(tab_side.at[1, 2], tab_in.at[8], 8, (x_row, c))
    tab_in[0] = tab_out[0]
    tab_in[2] = tab_side[0, 0]
    tab_in[3] = tab_side[1, 0]
    for piece, (first, count) in enumerate(GRID_PIECES):
        arrived(0, enc_halo, 2, first, count, piece)
        send(0, enc_halo, 2, 7, first, count, piece, (x_row, c), started)
        arrived(0, enc_halo, 3, first, count, piece)
        send(0, enc_halo, 3, 8, first, count, piece, (x_row, c), started)
    send(0, enc_halo, 2, 5, 0, G, 0, (partner, c), started)
    send(0, enc_halo, 3, 6, 0, G, 0, (partner, c), started)
    tab_copies[2].wait_recv()
    tab_copies[3].wait_recv()
    near = (0, 1, 2, 3, 4)
    tables(near, 0)
    enc_matrices(near, 0)
    for copy in weight_copies[0][1:]:
        copy.wait()
    arrived(0, enc_halo, 1, 0, G, 0)
    arrived(0, enc_halo, 4, 0, G, 0)
    messages(enc_halo, enc_w, CE, 0, near, msg)
    base[...] = dot(mesh_own[...], nf[0, 0])
    for copy in tab_copies[4:]:
        copy.wait_recv()
    diagonal = (5, 6, 7, 8)
    tables(diagonal, 1)
    enc_matrices(diagonal, 1)
    arrived(0, enc_halo, 5, 0, G, 0)
    arrived(0, enc_halo, 6, 0, G, 0)
    messages(enc_halo, enc_w, CE, 0, (5, 6), msg)
    agg[...] = dot(enc_m[:, 0 : 7 * CE], msg[0 : 7 * CE, :])

    proc_rows, proc_cols = slot_receivers(slot_pad[...], recv_pad[...], 24)
    for k in range(9):
        for half in range(2):
            receiver = pick(k, lambda b: proc_rows[2 * b + half : 2 * b + half + 1, :])
            first = k * CM + half * 128
            proc_m[:, first : first + 128] = ones_where(receiver == iota((N, 128), 0))
    proc_matrices(near, 0)
    dec_matrices()
    for copy in far_copies:
        copy.wait_recv()
    found = []
    for q in range(nc):
        number = far_in[q]
        device = number // CO
        band = device // nc
        index = (band % 2) * (nzx * CO) + (band // 2) * CO + number % CO
        index = jnp.where(device % nc == c, index, -1)
        found.append(
            jnp.concatenate(
                [ones_where(index == iota((FAR, 128), 1) + 128 * t) for t in range(max(1, nr * CO // 128))],
                axis=1,
            )
        )
    far_pick[...] = jnp.concatenate(found, axis=0)

    for k in (7, 8):
        for piece, (first, count) in enumerate(GRID_PIECES):
            arrived(0, enc_halo, k, first, count, piece)
    messages(enc_halo, enc_w, CE, 0, (7, 8), msg)
    ahead, pushes = finish_step(0, mesh_own[...], enc_m, 7 * CE, 9 * CE)
    for copy in started + tab_copies + far_copies:
        copy.wait_send()

    for s in range(2):
        i = s + 1
        halo = proc_halo.at[s]
        own = lat[...]
        started, peer_copies = ahead, pushes
        receiver_part = dot(own, ef[i, 1]).astype(BF)
        for k in range(9):
            halo[k, N : 2 * N, :] = receiver_part
        base[...] = dot(own, nf[i, 0])
        arrived(i, halo, 1, 0, N, 0)
        messages(halo, proc_w, CM, i, (0, 1), msg)
        for piece in range(3):
            arrived(i, halo, 2, piece * CH, CH, piece)
            send(i, halo, 2, 7, piece * CH, CH, piece, (x_row, c), started)
            arrived(i, halo, 3, piece * CH, CH, piece)
            send(i, halo, 3, 8, piece * CH, CH, piece, (x_row, c), started)
            if piece == 1:
                arrived(i, halo, 4, 3 * CH, CH, 3)
                send(i, halo, 4, 8, 3 * CH, CH, 3, (r, right), started)
                send(i, halo, 4, 7, 3 * CH, CH, 3, (r, left), started)
                for copy in peer_copies:
                    copy.wait_recv()
                mine = pl.ds(pl.multiple_of(core * (nzx * CO), CO), nzx * CO)
                to_partner = pltpu.make_async_remote_copy(
                    gath.at[s, mine], gath.at[s, mine], p_ss.at[s], p_rs.at[s],
                    device_id=(partner, c), device_id_type=MESH,
                )
                to_partner.start()
        to_partner.wait_recv()
        chosen = dot(far_pick[...], gath[s]).astype(BF)
        c_out[s] = chosen
        mate_copies = []
        for q in range(1, nc):
            copy = pltpu.make_async_remote_copy(
                c_out.at[s, pl.ds(q * FAR, FAR)], c_in.at[s, q], y_ss.at[s, q], y_rs.at[s, q],
                device_id=mate(q), device_id_type=MESH,
            )
            copy.start()
            mate_copies.append(copy)

        arrived(i, halo, 2, 3 * CH, CH, 3)
        send(i, halo, 2, 5, 0, N, 0, (partner, c), started)
        arrived(i, halo, 3, 3 * CH, CH, 3)
        send(i, halo, 3, 6, 0, N, 0, (partner, c), started)
        messages(halo, proc_w, CM, i, (2, 3), msg)
        if s == 0:
            proc_matrices(diagonal, 1)
        arrived(i, halo, 4, 0, 3 * CH, 0)
        for k in (5, 6):
            arrived(i, halo, k, 0, N, 0)
        messages(halo, proc_w, CM, i, (4, 5, 6), msg)
        agg[...] = dot(proc_m[:, 0 : 7 * CM], msg[0 : 7 * CM, :])
        pre = c_out[s, 0:FAR, :].astype(F32) + dot(far_e[...], halo[0, N : 2 * N, :])
        for copy in mate_copies:
            copy.wait_recv()
        for q in range(1, nc):
            pre = pre + c_in[s, q].astype(F32)
        for k in (7, 8):
            for piece in range(4):
                arrived(i, halo, k, piece * CH, CH, piece)
        messages(halo, proc_w, CM, i, (7, 8), msg, pre)
        ahead, pushes = finish_step(i, own, proc_m, 7 * CM, 9 * CM + FAR)
        for copy in started + peer_copies + mate_copies + [to_partner]:
            copy.wait_send()

    for copy in weight_copies[3]:
        copy.wait()
    sent = dot(lat[...], ef[3, 0]).astype(BF)
    dec_out[...] = dot(dec_g[...], sent).astype(BF)
    dec_copies = []
    for b in (0, 2, 6, 8, 1, 7, 3, 5):
        span = pl.ds(b * CD, CD)
        copy = pltpu.make_async_remote_copy(
            dec_out.at[span], dec_in.at[span], d_ss.at[b], d_rs.at[b],
            device_id=target(b), device_id_type=MESH,
        )
        copy.start()
        dec_copies.append(copy)
    dec_in[4 * CD : 5 * CD, :] = dec_out[4 * CD : 5 * CD, :]
    own = grid_lat[...]
    receiver_part = dot(own, ef[3, 1]).astype(BF)
    near = dot(dec_e[...], receiver_part)
    start = dot(own, nf[3, 0])
    for copy in dec_copies:
        copy.wait_recv()
    pre = dec_in[...].astype(F32) + near
    y = dot(silu(pre), es[3])
    message = layer_norm(y, edge_gain[3:4, :]).astype(BF)
    out_copy.wait()
    final = node_update(3, own, dot(dec_m[...], message), start)
    out[...] = grid_in[...].astype(F32) + dot_nt(out_own[...], final)
    for copy in dec_copies:
        copy.wait_send()


def on_device(nr, nc, *args):
    vmem = pl.BlockSpec(memory_space=pltpu.VMEM)
    hbm = pl.BlockSpec(memory_space=pl.ANY)
    in_specs = [hbm] * 21
    args = list(args)
    args[4] = args[4].reshape(1, L)
    args[0] = args[0].T
    args[11] = args[11].T
    for at in (12, 15, 18):
        args[at] = jnp.transpose(args[at], (1, 0, 2))
    dma = pltpu.SemaphoreType.DMA
    nzx = nr // 2
    prediction = pl.pallas_call(
        functools.partial(body, nr, nc),
        out_shape=jax.ShapeDtypeStruct((CIN, G), F32),
        in_specs=in_specs,
        out_specs=vmem,
        scratch_shapes=[
            pltpu.VMEM((9, 1, CE), I32),
            pltpu.VMEM((9, 1, CM), I32),
            pltpu.VMEM((CIN, G), BF),
            pltpu.VMEM((CIN, L), BF),
            pltpu.VMEM((L, L), BF),
            pltpu.VMEM((1, L), F32),
            pltpu.VMEM((1, EM), I32),
            pltpu.VMEM((1, EM), I32),
            pltpu.VMEM((1, EE), I32),
            pltpu.VMEM((1, EE), I32),
            pltpu.VMEM((4, L), F32),
            pltpu.VMEM((4, L), F32),
            pltpu.VMEM((9, 1, CD), I32),
            pltpu.VMEM((1, ED), I32),
            pltpu.VMEM((1, ED), I32),
            pltpu.VMEM((4, 2, L, L), BF),
            pltpu.VMEM((4, L, L), BF),
            pltpu.VMEM((4, 2, L, L), BF),
            pltpu.VMEM((4, L, L), BF),
            pltpu.VMEM((N, L), BF),
            pltpu.VMEM((CIN, L), BF),
            pltpu.VMEM((9, 8, 128), I32),
            pltpu.VMEM((9, 8, 128), I32),
            pltpu.VMEM((2, 3, 8, 128), I32),
            pltpu.VMEM((128, 128), F32),
            pltpu.VMEM((2, 128, 128), I32),
            pltpu.VMEM((FAR, 128), I32),
            pltpu.VMEM((nc, FAR, 128), I32),
            pltpu.VMEM((nc * FAR, nr * CO), BF),
            pltpu.VMEM((1, EMP), I32),
            pltpu.VMEM((1, EMP), I32),
            pltpu.VMEM((16, 128), I32),
            pltpu.VMEM((9, G + N, L), BF),
            pltpu.VMEM((9, CE, G + N), BF),
            pltpu.VMEM((N, 9 * CE), BF),
            pltpu.VMEM((2, 9, 2 * N, L), BF),
            pltpu.VMEM((9, CM, 2 * N), BF),
            pltpu.VMEM((N, 9 * CM + FAR), BF),
            pltpu.VMEM((FAR, N), BF),
            pltpu.VMEM((2, nr * CO, L), BF),
            pltpu.VMEM((2, nc * FAR, L), BF),
            pltpu.VMEM((2, nc, FAR, L), BF),
            pltpu.VMEM((9 * CD, L), BF),
            pltpu.VMEM((640, L), BF),
            pltpu.VMEM((9 * CD, N), BF),
            pltpu.VMEM((640, G), BF),
            pltpu.VMEM((G, 640), BF),
            pltpu.VMEM((G, L), BF),
            pltpu.VMEM((N, L), BF),
            pltpu.VMEM((N, L), F32),
            pltpu.VMEM((N, L), F32),
            pltpu.VMEM((9 * CM + FAR, L), BF),
            dma((5, 4)),
            dma((15,)),
            dma((9,)),
            dma((9,)),
            dma((nc,)),
            dma((nc,)),
            dma((3, 9, 4)),
            dma((3, 9, 4)),
            dma((2, nzx)),
            dma((2, nzx)),
            dma((2,)),
            dma((2,)),
            dma((2, nc)),
            dma((2, nc)),
            dma((9,)),
            dma((9,)),
        ],
        compiler_params=pltpu.CompilerParams(
            collective_id=0, has_side_effects=True, vmem_limit_bytes=60 * 1024 * 1024
        ),
    )(*args)
    return prediction.T


def solution(mesh):
    both = ("row", "col")
    placed = (
        (P(both, None),) * 2
        + (P(),) * 10
        + (P(both, None, None), P(both, None), P(both, None)) * 3
    )
    return jax.shard_map(
        functools.partial(on_device, mesh.shape["row"], mesh.shape["col"]),
        mesh=mesh,
        in_specs=placed,
        out_specs=P(both, None),
        check_vma=False,
    )
```
